256 devices in a mesh: ctx: 32 (over x_hi, z, core), head: 8 (over y, x_lo).
Axes of the slice: x: 4 (x_hi: 2, x_lo: 2; x = x_hi * 2 + x_lo), y: 4, z: 8, core: 2. Of those that a mesh axis runs over, the one named last changes fastest.
Arguments:
- patches: bfloat16 [5120, 4608], P('ctx'), may hold values from -6 to 6
- vis_pos: int32 [5120], P('ctx'), may hold values from 0 to 8191, as said below
- span_of: int32 [32, 2], P('ctx'), may hold values from 0 to 63, as said below
- text_rows: bfloat16 [8192, 4096], P('ctx', 'head'), may hold values from -250 to 250
- proj_weight: bfloat16 [4608, 4096], P(None, 'head'), may hold values from -0.09375 to 0.09375
- norm_gain: float32 [4096], replicated, may hold values from 0.1 to 1.9
- qkv_weight: bfloat16 [4096, 8, 6, 128], P(None, 'head'), may hold values from -3 to 3
Outputs:
- context: bfloat16 [8192, 4096], P('ctx', 'head')
The draws below stay inside these ranges and needn't reach their ends.
Inputs may be any that keep to these rules, and one draw needn't show every extreme that they name: vis_pos holds distinct positions. Span c is positions c * 128 to c * 128 + 127; at most 8 of the patch rows of one index of ctx lie in the two spans of one owner, and exactly 8 for one owner of each index. span_of lists every span number once.
All inputs are finite; a program needn't handle non-finite values.
Results may differ from the reference program's by a relative error of at most 0.012.
The reference program's roundings to bfloat16 on the way (of `visual`, `sequence`, `normed` and `weights`) count: a program that leaves them out, or rounds other values in their place, can miss the bound.
Values may be sent and summed in bfloat16 or wider, within the bound.
No kernel may reach another device: no remote copies, remote signals or barrier semaphores. Data moves between devices by JAX's collectives and lax.ppermute only.
A program may use at most 64 MiB of HBM per device.

```python
import math
import jax
import jax.numpy as jnp
from jax import lax

D = 4096
HEADS = 32
KVH = 8
HD = 128
VIS = 4608
S_DEV = 256
VIS_DEV = 160
TOKENS = 8192
NVIS = 5120


def span_layout(key):
    owners = TOKENS // S_DEV
    half_rows = S_DEV // 2
    capacity = S_DEV // owners
    span_key, ticket_key, favour_key, slot_key = jax.random.split(key, 4)
    span_table = jax.random.permutation(span_key, 2 * owners).astype(jnp.int32).reshape(owners, 2)
    tickets = owners * capacity

    def ticket_order(one_key):
        return jax.random.permutation(one_key, tickets).astype(jnp.int32)
    ranking = jax.vmap(ticket_order)(jax.random.split(ticket_key, owners))
    favoured = jax.random.randint(favour_key, (owners,), 0, owners).astype(jnp.int32)
    ticket_owner = jnp.arange(tickets, dtype=jnp.int32) // capacity
    priority = jnp.where(ticket_owner[None, :] == favoured[:, None], ranking - tickets, ranking)
    chosen = jnp.argsort(priority, axis=1, stable=True)[:, :VIS_DEV].astype(jnp.int32)
    flat_dest = (chosen // capacity).reshape(-1)
    onehot = (flat_dest[:, None] == jnp.arange(owners, dtype=jnp.int32)[None, :]).astype(jnp.int32)
    slot_rank = jnp.sum((jnp.cumsum(onehot, axis=0) - 1) * onehot, axis=1)

    def slot_order(one_key):
        return jax.random.permutation(one_key, S_DEV).astype(jnp.int32)
    slot_orders = jax.vmap(slot_order)(jax.random.split(slot_key, owners))
    local_slot = slot_orders[flat_dest, slot_rank]
    positions = span_table[flat_dest, local_slot // half_rows] * half_rows + local_slot % half_rows
    return (span_table, positions.astype(jnp.int32))


def draw_vis_pos(key, part):
    return span_layout(key)[1]


def draw_span_of(key, part):
    return span_layout(key)[0]


def draw_text_rows(key, part):
    key = jax.random.fold_in(key, 11)
    column_key, row_key, value_key = jax.random.split(key, 3)
    column_scale = jnp.exp(jax.random.uniform(column_key, (1, D), minval=0.0, maxval=math.log(10.0)))
    row_scale = jnp.exp(jax.random.uniform(row_key, (TOKENS, 1), minval=0.0, maxval=math.log(10.0)))
    base = jax.random.normal(value_key, (TOKENS, D))
    return (base * column_scale * row_scale * 0.3).astype(jnp.bfloat16)


def draw_qkv_weight(key, part):
    key = jax.random.fold_in(key, 23)
    groups = HEADS // KVH
    entries = jax.random.normal(key, (D, KVH, groups + 2, HD))
    column_scale = jnp.where(jnp.arange(groups + 2) < groups + 1, 1.6, 1.0).astype(jnp.float32)
    weights = entries * column_scale[None, None, :, None] * D ** (-0.5)
    weights = jnp.clip(weights, -3.0, 3.0)
    return weights.astype(jnp.bfloat16)


def block_levels(key, shape, cuts, least, largest):
    loudness, own = 1.0, jax.random.fold_in(key, 6)
    for dim, shards_of in cuts:
        steps = jnp.exp(jax.random.uniform(jax.random.fold_in(own, dim), (shards_of,), jnp.float32, least / len(cuts), largest / len(cuts)))
        loudness = loudness * jnp.repeat(steps, shape[dim] // shards_of).reshape([-1 if axis == dim else 1 for axis in range(len(shape))])
    return loudness


def bell_draw(rng, shape, width, most, cuts=(), kind=jnp.bfloat16):
    values = width * jax.random.normal(rng, shape, jnp.float32)
    if cuts:
        values = values * block_levels(rng, shape, cuts, -0.22, 0.18)
    return jnp.clip(values, -most, most).astype(kind)


def setup_inputs(seed: int = 0) -> dict:
    streams_of = jax.random.split(jax.random.key(seed), 8)
    return {
        "patches": bell_draw(streams_of[0], (NVIS, VIS), 1.0, 6.0, ((0, 32),)),
        "vis_pos": draw_vis_pos(jax.random.fold_in(streams_of[7], 71), 0),
        "span_of": draw_span_of(jax.random.fold_in(streams_of[7], 71), 0),
        "text_rows": draw_text_rows(jax.random.fold_in(streams_of[7], 71), 0),
        "proj_weight": bell_draw(streams_of[4], (VIS, D), VIS ** -0.5, 0.09375, ((1, 8),)),
        "norm_gain": jnp.clip(1.0 + 0.18 * jax.random.normal(streams_of[5], (D,), jnp.float32), 0.1, 1.9),
        "qkv_weight": draw_qkv_weight(jax.random.fold_in(streams_of[7], 71), 0),
    }


rope_theta = 500000.0
norm_eps = 1e-05
masked_score = -1e+30

def apply_rotary(vectors, positions):
    head_size = vectors.shape[-1]
    frequency = rope_theta ** (-jnp.arange(0, head_size, 2, dtype=jnp.float32) / head_size)
    angles = positions.astype(jnp.float32)[:, None] * frequency[None, :]
    angles = jnp.concatenate([angles, angles], axis=-1)
    view_shape = (positions.shape[0],) + (1,) * (vectors.ndim - 2) + (head_size,)
    cosine = jnp.cos(angles).reshape(view_shape)
    sine_part = jnp.sin(angles).reshape(view_shape)
    half_size = head_size // 2
    turned = jnp.concatenate([-vectors[..., half_size:], vectors[..., :half_size]], axis=-1)
    return vectors * cosine + turned * sine_part

def reference(patches, vis_pos, span_of, text_rows, proj_weight, norm_gain, qkv_weight):
    half_rows = S_DEV // 2
    groups = HEADS // KVH
    visual = jnp.dot(patches, proj_weight, preferred_element_type=jnp.float32).astype(jnp.bfloat16)
    local_rows = jnp.arange(S_DEV, dtype=jnp.int32)
    row_position = (span_of[:, local_rows // half_rows] * half_rows + (local_rows % half_rows)[None, :]).reshape(TOKENS).astype(jnp.int32)
    sequence = jnp.zeros((TOKENS, D), jnp.bfloat16).at[row_position].set(text_rows)
    sequence = sequence.at[vis_pos].set(visual)
    wide = sequence.astype(jnp.float32)
    squares = lax.optimization_barrier(jnp.mean(wide * wide, axis=-1, keepdims=True))
    normed = (wide * lax.rsqrt(squares + norm_eps) * norm_gain.astype(jnp.float32)[None, :]).astype(jnp.bfloat16)
    projected = jnp.dot(normed, qkv_weight.reshape(D, KVH * (groups + 2) * HD), preferred_element_type=jnp.float32)
    projected = projected.reshape(TOKENS, KVH, groups + 2, HD)
    positions = jnp.arange(TOKENS, dtype=jnp.int32)
    queries = apply_rotary(projected[:, :, :groups], positions).astype(jnp.bfloat16)
    key_rows = apply_rotary(projected[:, :, groups], positions).astype(jnp.bfloat16)
    value_rows = projected[:, :, groups + 1].astype(jnp.bfloat16)
    heads_all = KVH * groups
    query_heads = queries.reshape(TOKENS, heads_all, HD).transpose(1, 0, 2)
    key_heads = key_rows.transpose(1, 0, 2)
    value_heads = value_rows.transpose(1, 0, 2)
    head_owner = jnp.arange(heads_all, dtype=jnp.int32) // groups
    score_scale = HD ** (-0.5)
    block_count = TOKENS // half_rows

    def one_head(element):
        query_head, kv_index = element
        key_head = key_heads[kv_index]
        value_head = value_heads[kv_index]

        def one_block(first_row):
            block_queries = lax.dynamic_slice_in_dim(query_head, first_row, half_rows, 0)
            scores = jnp.dot(block_queries, key_head.T, preferred_element_type=jnp.float32) * score_scale
            query_pos = first_row + jnp.arange(half_rows, dtype=jnp.int32)
            allowed = positions[None, :] <= query_pos[:, None]
            scores = jnp.where(allowed, scores, masked_score)
            row_top = lax.optimization_barrier(jnp.max(scores, axis=-1, keepdims=True))
            exp_terms = jnp.exp(scores - row_top)
            row_total = lax.optimization_barrier(jnp.sum(exp_terms, axis=-1, keepdims=True))
            weights = exp_terms.astype(jnp.bfloat16)
            return jnp.dot(weights, value_head, preferred_element_type=jnp.float32) / row_total
        starts = jnp.arange(block_count, dtype=jnp.int32) * half_rows
        return lax.map(one_block, starts).reshape(TOKENS, HD)
    attended = lax.map(one_head, (query_heads, head_owner))
    combined = attended.transpose(1, 0, 2).reshape(TOKENS, heads_all * HD)
    return combined[row_position].astype(jnp.bfloat16)
```

```python
import functools
import math

import jax
import jax.numpy as jnp
from jax import lax
from jax.experimental import pallas as pl
from jax.experimental.pallas import tpu as pltpu
from jax.sharding import PartitionSpec as P

HEADS = 32
KVH = 8
HD = 128
GROUPS = HEADS // KVH
WIDE = (GROUPS + 2) * HD
SPAN = 128
ROWS = 2 * SPAN
OWNERS = 32
CAP = ROWS // OWNERS
SLOTS = OWNERS * CAP
Z = 8
Y = 4
HEAD_DEVS = 8
COLS = 512
MAIL = WIDE + HD
QCOLS = GROUPS * ROWS
STATE = HD + 8

rope_theta = 500000.0
norm_eps = 1e-05
masked_score = -1e30
EXP_SCALE = HD ** (-0.5) * math.log2(math.e)
VMEM_LIMIT = 56 * 1024 * 1024

bf16 = jnp.bfloat16
f32 = jnp.float32


def ctx_perm(move):
    return [(i, move(i)) for i in range(OWNERS)]


def z_shift(step):
    return ctx_perm(lambda i: (i // 16) * 16 + ((i // 2 % Z + step) % Z) * 2 + i % 2)


def core_swap():
    return ctx_perm(lambda i: i ^ 1)


def xhi_swap():
    return ctx_perm(lambda i: i ^ 16)


def y_shift(step):
    return [(i, (i // 2 + step) % Y * 2 + i % 2) for i in range(HEAD_DEVS)]


def xlo_swap():
    return [(i, i ^ 1) for i in range(HEAD_DEVS)]


def rotary_tables(positions):
    frequency = rope_theta ** (-jnp.arange(0, HD, 2, dtype=f32) / HD)
    angles = positions.astype(f32)[:, None] * frequency[None, :]
    cosine, sine = jnp.cos(angles), jnp.sin(angles)
    return jnp.concatenate([cosine, cosine], axis=1), jnp.concatenate([-sine, sine], axis=1)


def head_gather(own):
    half = own.shape[0] // 2
    side = lax.ppermute(own, "head", xlo_swap())
    down = lax.ppermute(own, "head", y_shift(1))
    up = lax.ppermute(own, "head", y_shift(-1))
    far = lax.ppermute(down, "head", y_shift(1))
    side_up = lax.ppermute(side, "head", y_shift(-1))
    side_down = lax.ppermute(down, "head", xlo_swap())
    far_top = lax.ppermute(side_down[:half], "head", y_shift(1))
    far_low = lax.ppermute(side_up[half:], "head", y_shift(-1))
    return [own, side, down, up, far, side_up, side_down, far_top, far_low]


def block_order():
    place = lax.axis_index("head")
    y, x = place // 2, place % 2

    def at(step, flip):
        return (y + step) % Y * 2 + (x + flip) % 2

    order = [at(0, 0), at(0, 1), at(-1, 0), at(1, 0), at(2, 0), at(1, 1), at(-1, 1), at(2, 1)]
    return jnp.stack(order).astype(jnp.int32)


def qkv_kernel(rows, send, *refs):
    order_ref = refs[0]
    blocks = refs[1:10]
    weight_ref, gain_ref, cos_ref, sin_ref = refs[10:14]
    half = rows // 2

    def block(k):
        if k < 7:
            return blocks[k][...].astype(f32)
        return jnp.concatenate([blocks[7][...], blocks[8][...]], axis=0).astype(f32)

    total = jnp.zeros((rows, 1), f32)
    for k in range(8):
        wide = block(k)
        total = total + jnp.sum(wide * wide, axis=1, keepdims=True)
    inverse = lax.rsqrt(total * (1.0 / (8 * COLS)) + norm_eps)
    projected = jnp.zeros((rows, WIDE), f32)
    for k in range(8):
        normed = (block(k) * inverse * gain_ref[order_ref[k]]).astype(bf16)
        projected = projected + jnp.dot(
            normed, weight_ref[order_ref[k]], preferred_element_type=f32
        )
    cosine, sine = cos_ref[...], sin_ref[...]
    parts = []
    for j in range(GROUPS + 2):
        slab = projected[:, j * HD : (j + 1) * HD]
        if j <= GROUPS:
            slab = slab * cosine + pltpu.roll(slab, HD // 2, 1) * sine
        parts.append(slab.astype(bf16))
    if not send:
        out_ref = refs[14]
        for j in range(GROUPS + 2):
            out_ref[:, j * HD : (j + 1) * HD] = parts[j]
        return
    slot_ref, mark_ref, out_ref = refs[14:17]
    places = lax.broadcasted_iota(jnp.int32, (SLOTS, rows), 0)
    pick = jnp.where(places == slot_ref[...], 1.0, 0.0).astype(bf16)
    parts.append(mark_ref[...])
    for j in range(GROUPS + 3):
        out_ref[:, j * HD : (j + 1) * HD] = jnp.dot(
            pick, parts[j], preferred_element_type=f32
        ).astype(bf16)


def vmem(count):
    return [pl.BlockSpec(memory_space=pltpu.VMEM)] * count


def smem(count):
    return [pl.BlockSpec(memory_space=pltpu.SMEM)] * count


def project_qkv(order, blocks, weight, gain, cosine, sine, slots=None, marks=None):
    rows = blocks[0].shape[0]
    send = slots is not None
    extra = (slots, marks) if send else ()
    return pl.pallas_call(
        functools.partial(qkv_kernel, rows, send),
        out_shape=jax.ShapeDtypeStruct((SLOTS, MAIL) if send else (rows, WIDE), bf16),
        in_specs=smem(1) + vmem(13 + len(extra)),
        out_specs=pl.BlockSpec(memory_space=pltpu.VMEM),
        compiler_params=pltpu.CompilerParams(vmem_limit_bytes=VMEM_LIMIT),
        cost_estimate=pl.CostEstimate(
            flops=2 * rows * 8 * COLS * WIDE, bytes_accessed=8 * COLS * WIDE * 2 + rows * 8192, transcendentals=0
        ),
        name="norm_qkv",
    )(order, *blocks, weight, gain, cosine, sine, *extra)


def merge_kernel(mail_ref, text_ref, query_ref, kv_ref):
    mail = mail_ref[...]
    marks = mail[:, WIDE : WIDE + 1].astype(f32)
    rows = (lax.broadcasted_iota(jnp.int32, (SLOTS, ROWS), 1) + 1).astype(f32)
    place = jnp.where(marks == rows, 1.0, 0.0).astype(bf16)
    placed = lax.dot_general(place, mail, (((0,), (0,)), ((), ())), preferred_element_type=f32)
    visual = placed[:, WIDE:] > 0.5
    for j in range(GROUPS + 2):
        cols = slice(j * HD, (j + 1) * HD)
        slab = jnp.where(visual, placed[:, cols], text_ref[:, cols].astype(f32))
        if j == GROUPS:
            kv_ref[:ROWS, :] = slab.astype(bf16)
            continue
        for s in range(2):
            turned = slab[s * SPAN : (s + 1) * SPAN, :].T.astype(bf16)
            if j < GROUPS:
                start = (s * GROUPS + j) * SPAN
                query_ref[:, start : start + SPAN] = turned
            else:
                kv_ref[ROWS + s * SPAN : ROWS + (s + 1) * SPAN, :] = turned


def merge_rows(mail, text):
    return pl.pallas_call(
        merge_kernel,
        out_shape=(
            jax.ShapeDtypeStruct((HD, QCOLS), bf16),
            jax.ShapeDtypeStruct((2 * ROWS, HD), bf16),
        ),
        in_specs=vmem(2),
        out_specs=tuple(vmem(2)),
        compiler_params=pltpu.CompilerParams(vmem_limit_bytes=VMEM_LIMIT),
        cost_estimate=pl.CostEstimate(
            flops=2 * SLOTS * ROWS * MAIL, bytes_accessed=4 * ROWS * MAIL, transcendentals=0
        ),
        name="merge_rows",
    )(mail, text)


def attend_kernel(first, offsets, *refs):
    count = len(offsets)
    table_ref, place_ref = refs[:2]
    query_refs = refs[2:4]
    kv_refs = refs[4 : 4 + count]
    outs = refs[-2:]
    if first:
        for out in outs:
            out[:HD, :] = jnp.zeros((HD, QCOLS), f32)
            out[HD : HD + 1, :] = jnp.full((1, QCOLS), masked_score, f32)
            out[HD + 1 : STATE, :] = jnp.zeros((STATE - HD - 1, QCOLS), f32)
    else:
        ins = refs[4 + count : 6 + count]
        for given, out in zip(ins, outs):
            out[...] = given[...]
    x_hi, z, core = place_ref[0], place_ref[1], place_ref[2]
    key_spans = []
    for flip, step in offsets:
        source = ((x_hi + flip) % 2 * Z + (z + step + Z) % Z) * 2 + core
        key_spans.append((table_ref[2 * source], table_ref[2 * source + 1]))
    here = (x_hi * Z + z) * 2
    row_in_span = lax.broadcasted_iota(jnp.int32, (SPAN, 1), 0)
    lane = lax.broadcasted_iota(jnp.int32, (1, GROUPS * SPAN), 1) % SPAN
    for half in range(2):
        owner = here + (core + half) % 2
        for s in range(2):
            query_span = table_ref[2 * owner + s]
            query_pos = query_span * SPAN + lane
            cols = slice(s * GROUPS * SPAN, (s + 1) * GROUPS * SPAN)
            out = outs[half]
            lowest = functools.reduce(jnp.minimum, [k for pair in key_spans for k in pair])

            @pl.when(lowest <= query_span)
            def _():
                queries = query_refs[half][:, cols]
                top = out[HD : HD + 1, cols]
                scores = []
                new_top = top
                for b in range(count):
                    score = jnp.dot(kv_refs[b][:ROWS, :], queries, preferred_element_type=f32)
                    key_pos = jnp.concatenate(
                        [key_spans[b][0] * SPAN + row_in_span, key_spans[b][1] * SPAN + row_in_span],
                        axis=0,
                    )
                    score = jnp.where(key_pos <= query_pos, score, masked_score)
                    new_top = jnp.maximum(new_top, jnp.max(score, axis=0, keepdims=True))
                    scores.append(score)
                shrink = jnp.exp2((top - new_top) * EXP_SCALE)
                total = out[HD + 1 : HD + 2, cols] * shrink
                accum = out[:HD, cols] * shrink
                for b in range(count):
                    terms = jnp.exp2((scores[b] - new_top) * EXP_SCALE)
                    total = total + jnp.sum(terms, axis=0, keepdims=True)
                    turned = jnp.concatenate(
                        [kv_refs[b][ROWS : ROWS + SPAN, :], kv_refs[b][ROWS + SPAN :, :]], axis=1
                    )
                    accum = accum + jnp.dot(
                        turned, terms.astype(bf16), preferred_element_type=f32
                    )
                out[:HD, cols] = accum
                out[HD : HD + 1, cols] = new_top
                out[HD + 1 : HD + 2, cols] = total


def attend(table, place, queries, blocks, offsets, states):
    first = states is None
    count = len(blocks)
    given = () if first else tuple(states)
    return pl.pallas_call(
        functools.partial(attend_kernel, first, offsets),
        out_shape=(jax.ShapeDtypeStruct((STATE, QCOLS), f32),) * 2,
        in_specs=smem(2) + vmem(2 + count + len(given)),
        out_specs=tuple(vmem(2)),
        compiler_params=pltpu.CompilerParams(vmem_limit_bytes=VMEM_LIMIT),
        cost_estimate=pl.CostEstimate(
            flops=4 * count * ROWS * 2 * QCOLS * HD,
            bytes_accessed=count * 4 * ROWS * HD + 2 * STATE * QCOLS * 8,
            transcendentals=count * ROWS * 2 * QCOLS,
        ),
        name="attend",
    )(table, place, *queries, *blocks, *given)


def finish_kernel(mine_ref, theirs_ref, out_ref):
    top_a, top_b = mine_ref[HD : HD + 1, :], theirs_ref[HD : HD + 1, :]
    top = jnp.maximum(top_a, top_b)
    scale_a = jnp.exp2((top_a - top) * EXP_SCALE)
    scale_b = jnp.exp2((top_b - top) * EXP_SCALE)
    total = mine_ref[HD + 1 : HD + 2, :] * scale_a + theirs_ref[HD + 1 : HD + 2, :] * scale_b
    accum = (mine_ref[:HD, :] * scale_a + theirs_ref[:HD, :] * scale_b) / total
    for s in range(2):
        for g in range(GROUPS):
            start = (s * GROUPS + g) * SPAN
            out_ref[s * SPAN : (s + 1) * SPAN, g * HD : (g + 1) * HD] = accum[
                :, start : start + SPAN
            ].T.astype(bf16)


def finish(mine, theirs):
    return pl.pallas_call(
        finish_kernel,
        out_shape=jax.ShapeDtypeStruct((ROWS, GROUPS * HD), bf16),
        in_specs=vmem(2),
        out_specs=pl.BlockSpec(memory_space=pltpu.VMEM),
        compiler_params=pltpu.CompilerParams(vmem_limit_bytes=VMEM_LIMIT),
        name="finish",
    )(mine, theirs)


def on_device(patches, vis_pos, span_of, text_rows, proj_weight, norm_gain, qkv_weight):
    place = lax.axis_index("ctx")
    table = lax.all_to_all(
        jnp.broadcast_to(span_of[:, None, :], (OWNERS, 1, 2)), "ctx", split_axis=0, concat_axis=0, tiled=True
    ).reshape(2 * OWNERS)
    order = block_order()
    weight = qkv_weight.reshape(HEAD_DEVS, COLS, WIDE)
    gain = norm_gain.reshape(HEAD_DEVS, 1, COLS)

    visual = jnp.dot(patches, proj_weight, preferred_element_type=f32).astype(bf16)
    visual_blocks = head_gather(visual)
    text_blocks = head_gather(text_rows)

    matches = table[None, :] == (vis_pos // SPAN)[:, None]
    entry = jnp.sum(jnp.where(matches, jnp.arange(2 * OWNERS, dtype=jnp.int32)[None, :], 0), axis=1)
    owner = entry // 2
    count = vis_pos.shape[0]
    before = jnp.arange(count)[None, :] < jnp.arange(count)[:, None]
    rank = jnp.sum((owner[:, None] == owner[None, :]) & before, axis=1, dtype=jnp.int32)
    slots = (owner * CAP + rank)[None, :]
    marks = (entry % 2 * SPAN + vis_pos % SPAN + 1).astype(bf16)
    marks = jnp.broadcast_to(marks[:, None], (count, HD))

    vis_cos, vis_sin = rotary_tables(vis_pos)
    my_spans = span_of.reshape(2)
    row_pos = (my_spans[:, None] * SPAN + jnp.arange(SPAN, dtype=jnp.int32)[None, :]).reshape(ROWS)
    text_cos, text_sin = rotary_tables(row_pos)

    mail = project_qkv(order, visual_blocks, weight, gain, vis_cos, vis_sin, slots, marks)
    mail = lax.all_to_all(
        mail.reshape(OWNERS, CAP, MAIL), "ctx", split_axis=0, concat_axis=0, tiled=True
    ).reshape(SLOTS, MAIL)
    text_qkv = project_qkv(order, text_blocks, weight, gain, text_cos, text_sin)
    queries, own = merge_rows(mail, text_qkv)

    swap, forth, back = xhi_swap(), z_shift(1), z_shift(-1)
    across = lax.ppermute(own, "ctx", swap)
    other_queries = lax.ppermute(queries, "ctx", core_swap())
    both = (queries, other_queries)
    where = jnp.stack([place // 16, place // 2 % Z, place % 2]).astype(jnp.int32)
    step = functools.partial(attend, table, where, both)
    f_own, b_own = own, own
    f_across, b_across = across, across
    states = step([own], [(0, 0)], None)
    states = step([across], [(1, 0)], states)
    for hop in range(1, 5):
        f_own = lax.ppermute(f_own, "ctx", forth)
        f_across = lax.ppermute(f_across, "ctx", forth)
        if hop < 4:
            b_own = lax.ppermute(b_own, "ctx", back)
            b_across = lax.ppermute(b_across, "ctx", back)
            states = step([f_own, b_own], [(0, -hop), (0, hop)], states)
            states = step([f_across, b_across], [(1, -hop), (1, hop)], states)
        else:
            states = step([f_own, f_across], [(0, -hop), (1, -hop)], states)
    mine, others = states
    theirs = lax.ppermute(others, "ctx", core_swap())
    return finish(mine, theirs)


def solution(mesh):
    in_specs = (
        P("ctx", None),
        P("ctx"),
        P("ctx", None),
        P("ctx", "head"),
        P(None, "head"),
        P(),
        P(None, "head", None, None),
    )
    out_specs = P("ctx", "head")
    return jax.shard_map(
        on_device, mesh=mesh, in_specs=in_specs, out_specs=out_specs, check_vma=False
    )
```

```python
import functools
import math

import jax
import jax.numpy as jnp
from jax import lax
from jax.experimental import pallas as pl
from jax.experimental.pallas import tpu as pltpu
from jax.sharding import PartitionSpec as P

HEADS = 32
KVH = 8
HD = 128
GROUPS = HEADS // KVH
WIDE = (GROUPS + 2) * HD
SPAN = 128
ROWS = 2 * SPAN
OWNERS = 32
CAP = ROWS // OWNERS
SLOTS = OWNERS * CAP
Z = 8
Y = 4
HEAD_DEVS = 8
COLS = 512
MAIL = WIDE + HD
QCOLS = GROUPS * ROWS
STATE = HD + 8

rope_theta = 500000.0
norm_eps = 1e-05
masked_score = -1e30
EXP_SCALE = HD ** (-0.5) * math.log2(math.e)
VMEM_LIMIT = 16 * 1024 * 1024
ATTEND_LIMIT = 8 * 1024 * 1024
TILE = 128

bf16 = jnp.bfloat16
f32 = jnp.float32


def ctx_perm(move):
    return [(i, move(i)) for i in range(OWNERS)]


def z_shift(step):
    return ctx_perm(lambda i: (i // 16) * 16 + ((i // 2 % Z + step) % Z) * 2 + i % 2)


def core_swap():
    return ctx_perm(lambda i: i ^ 1)


def xhi_swap():
    return ctx_perm(lambda i: i ^ 16)


def y_shift(step):
    return [(i, (i // 2 + step) % Y * 2 + i % 2) for i in range(HEAD_DEVS)]


def xlo_swap():
    return [(i, i ^ 1) for i in range(HEAD_DEVS)]


def rotary_tables(positions):
    frequency = rope_theta ** (-jnp.arange(0, HD, 2, dtype=f32) / HD)
    angles = positions.astype(f32)[:, None] * frequency[None, :]
    cosine, sine = jnp.cos(angles), jnp.sin(angles)
    return jnp.concatenate([cosine, cosine], axis=1), jnp.concatenate([-sine, sine], axis=1)


def head_gather(own):
    half = own.shape[0] // 2
    side = lax.ppermute(own, "head", xlo_swap())
    down = lax.ppermute(own, "head", y_shift(1))
    up = lax.ppermute(own, "head", y_shift(-1))
    far = lax.ppermute(down, "head", y_shift(1))
    side_up = lax.ppermute(side, "head", y_shift(-1))
    side_down = lax.ppermute(down, "head", xlo_swap())
    far_top = lax.ppermute(side_down[:half], "head", y_shift(1))
    far_low = lax.ppermute(side_up[half:], "head", y_shift(-1))
    return [own, side, down, up, far, side_up, side_down, far_top, far_low]


def block_order():
    place = lax.axis_index("head")
    y, x = place // 2, place % 2

    def at(step, flip):
        return (y + step) % Y * 2 + (x + flip) % 2

    order = [at(0, 0), at(0, 1), at(-1, 0), at(1, 0), at(2, 0), at(1, 1), at(-1, 1), at(2, 1)]
    return jnp.stack(order).astype(jnp.int32)


def qkv_kernel(rows, send, *refs):
    order_ref = refs[0]
    blocks = refs[1:10]
    weight_ref, gain_ref, cos_ref, sin_ref = refs[10:14]
    half = rows // 2

    def block(k):
        if k < 7:
            return blocks[k][...].astype(f32)
        return jnp.concatenate([blocks[7][...], blocks[8][...]], axis=0).astype(f32)

    total = jnp.zeros((rows, 1), f32)
    for k in range(8):
        wide = block(k)
        total = total + jnp.sum(wide * wide, axis=1, keepdims=True)
    inverse = lax.rsqrt(total * (1.0 / (8 * COLS)) + norm_eps)
    pairs = (GROUPS + 2) // 2
    projected = [jnp.zeros((rows, 2 * HD), f32) for pair in range(pairs)]
    for k in range(8):
        place = order_ref[k]
        normed = (block(k) * inverse * gain_ref[place]).astype(bf16)
        for pair in range(pairs):
            weight = jnp.concatenate(
                [weight_ref[2 * pair, place], weight_ref[2 * pair + 1, place]], axis=1
            )
            projected[pair] = projected[pair] + jnp.dot(
                normed, weight, preferred_element_type=f32
            )
    cosine, sine = cos_ref[...], sin_ref[...]
    parts = []
    for j in range(GROUPS + 2):
        slab = projected[j // 2][:, j % 2 * HD : (j % 2 + 1) * HD]
        if j <= GROUPS:
            slab = slab * cosine + pltpu.roll(slab, HD // 2, 1) * sine
        parts.append(slab.astype(bf16))
    if not send:
        out_ref = refs[14]
        for j in range(GROUPS + 2):
            out_ref[:, j * HD : (j + 1) * HD] = parts[j]
        return
    slot_ref, mark_ref, out_ref = refs[14:17]
    places = lax.broadcasted_iota(jnp.int32, (SLOTS, rows), 0)
    pick = jnp.where(places == slot_ref[...], 1.0, 0.0).astype(bf16)
    parts.append(mark_ref[...])
    for j in range(GROUPS + 3):
        out_ref[:, j * HD : (j + 1) * HD] = jnp.dot(
            pick, parts[j], preferred_element_type=f32
        ).astype(bf16)


def vmem(count):
    return [pl.BlockSpec(memory_space=pltpu.VMEM)] * count


def smem(count):
    return [pl.BlockSpec(memory_space=pltpu.SMEM)] * count


def project_qkv(order, blocks, weight, gain, cosine, sine, slots=None, marks=None):
    rows = blocks[0].shape[0]
    send = slots is not None
    extra = (slots, marks) if send else ()
    return pl.pallas_call(
        functools.partial(qkv_kernel, rows, send),
        out_shape=jax.ShapeDtypeStruct((SLOTS, MAIL) if send else (rows, WIDE), bf16),
        in_specs=smem(1) + vmem(13 + len(extra)),
        out_specs=pl.BlockSpec(memory_space=pltpu.VMEM),
        compiler_params=pltpu.CompilerParams(vmem_limit_bytes=VMEM_LIMIT),
        cost_estimate=pl.CostEstimate(
            flops=2 * rows * 8 * COLS * WIDE, bytes_accessed=8 * COLS * WIDE * 2 + rows * 8192, transcendentals=0
        ),
        name="norm_qkv",
    )(order, *blocks, weight, gain, cosine, sine, *extra)


def merge_kernel(mail_ref, text_ref, query_ref, kv_ref):
    mail = mail_ref[...]
    marks = mail[:, WIDE : WIDE + 1].astype(f32)
    rows = (lax.broadcasted_iota(jnp.int32, (SLOTS, ROWS), 1) + 1).astype(f32)
    place = jnp.where(marks == rows, 1.0, 0.0).astype(bf16)
    placed = lax.dot_general(place, mail, (((0,), (0,)), ((), ())), preferred_element_type=f32)
    visual = placed[:, WIDE:] > 0.5
    for j in range(GROUPS + 2):
        cols = slice(j * HD, (j + 1) * HD)
        slab = jnp.where(visual, placed[:, cols], text_ref[:, cols].astype(f32))
        if j == GROUPS:
            kv_ref[:ROWS, :] = slab.astype(bf16)
            continue
        for s in range(2):
            turned = slab[s * SPAN : (s + 1) * SPAN, :].T.astype(bf16)
            if j < GROUPS:
                start = (s * GROUPS + j) * SPAN
                query_ref[:, start : start + SPAN] = turned
            else:
                kv_ref[ROWS + s * SPAN : ROWS + (s + 1) * SPAN, :] = turned


def merge_rows(mail, text):
    return pl.pallas_call(
        merge_kernel,
        out_shape=(
            jax.ShapeDtypeStruct((HD, QCOLS), bf16),
            jax.ShapeDtypeStruct((2 * ROWS, HD), bf16),
        ),
        in_specs=vmem(2),
        out_specs=tuple(vmem(2)),
        compiler_params=pltpu.CompilerParams(vmem_limit_bytes=VMEM_LIMIT),
        cost_estimate=pl.CostEstimate(
            flops=2 * SLOTS * ROWS * MAIL, bytes_accessed=4 * ROWS * MAIL, transcendentals=0
        ),
        name="merge_rows",
    )(mail, text)


def attend_kernel(first, offsets, *refs):
    count = len(offsets)
    table_ref, place_ref = refs[:2]
    query_refs = refs[2:4]
    kv_refs = refs[4 : 4 + count]
    outs = refs[-2:]
    if first:
        for out in outs:
            out[:HD, :] = jnp.zeros((HD, QCOLS), f32)
            out[HD : HD + 1, :] = jnp.full((1, QCOLS), masked_score, f32)
            out[HD + 1 : STATE, :] = jnp.zeros((STATE - HD - 1, QCOLS), f32)
    else:
        ins = refs[4 + count : 6 + count]
        for given, out in zip(ins, outs):
            out[...] = given[...]
    x_hi, z, core = place_ref[0], place_ref[1], place_ref[2]
    key_spans = []
    for flip, step in offsets:
        source = ((x_hi + flip) % 2 * Z + (z + step + Z) % Z) * 2 + core
        key_spans.append((table_ref[2 * source], table_ref[2 * source + 1]))
    here = (x_hi * Z + z) * 2
    row_in_span = lax.broadcasted_iota(jnp.int32, (SPAN, 1), 0)
    lane = lax.broadcasted_iota(jnp.int32, (1, TILE), 1)
    lowest = functools.reduce(jnp.minimum, [k for pair in key_spans for k in pair])
    for half in range(2):
        owner = here + (core + half) % 2
        out = outs[half]
        for s in range(2):
            query_span = table_ref[2 * owner + s]

            @pl.when(lowest <= query_span)
            def _():
                query_pos = query_span * SPAN + lane
                key_pos = [
                    jnp.concatenate([k * SPAN + row_in_span for k in pair], axis=0) for pair in key_spans
                ]
                values = [
                    jnp.concatenate([kv[ROWS : ROWS + SPAN, :], kv[ROWS + SPAN :, :]], axis=1) for kv in kv_refs
                ]
                for g in range(GROUPS):
                    start = (s * GROUPS + g) * SPAN
                    cols = slice(start, start + TILE)
                    queries = query_refs[half][:, cols]
                    top = out[HD : HD + 1, cols]
                    new_top = top
                    scores = []
                    for b in range(count):
                        score = jnp.dot(kv_refs[b][:ROWS, :], queries, preferred_element_type=f32)
                        score = jnp.where(key_pos[b] <= query_pos, score, masked_score)
                        new_top = jnp.maximum(new_top, jnp.max(score, axis=0, keepdims=True))
                        scores.append(score)
                    shrink = jnp.exp2((top - new_top) * EXP_SCALE)
                    total = out[HD + 1 : HD + 2, cols] * shrink
                    accum = out[:HD, cols] * shrink
                    for b in range(count):
                        terms = jnp.exp2((scores[b] - new_top) * EXP_SCALE)
                        total = total + jnp.sum(terms, axis=0, keepdims=True)
                        accum = accum + jnp.dot(values[b], terms.astype(bf16), preferred_element_type=f32)
                    out[:HD, cols] = accum
                    out[HD : HD + 1, cols] = new_top
                    out[HD + 1 : HD + 2, cols] = total


def attend(table, place, queries, blocks, offsets, states):
    first = states is None
    count = len(blocks)
    given = () if first else tuple(states)
    return pl.pallas_call(
        functools.partial(attend_kernel, first, offsets),
        out_shape=(jax.ShapeDtypeStruct((STATE, QCOLS), f32),) * 2,
        in_specs=smem(2) + vmem(2 + count + len(given)),
        out_specs=tuple(vmem(2)),
        compiler_params=pltpu.CompilerParams(vmem_limit_bytes=ATTEND_LIMIT),
        cost_estimate=pl.CostEstimate(
            flops=4 * count * ROWS * 2 * QCOLS * HD,
            bytes_accessed=count * 4 * ROWS * HD + 2 * STATE * QCOLS * 8,
            transcendentals=count * ROWS * 2 * QCOLS,
        ),
        name="attend",
    )(table, place, *queries, *blocks, *given)


def finish_kernel(mine_ref, theirs_ref, out_ref):
    top_a, top_b = mine_ref[HD : HD + 1, :], theirs_ref[HD : HD + 1, :]
    top = jnp.maximum(top_a, top_b)
    scale_a = jnp.exp2((top_a - top) * EXP_SCALE)
    scale_b = jnp.exp2((top_b - top) * EXP_SCALE)
    total = mine_ref[HD + 1 : HD + 2, :] * scale_a + theirs_ref[HD + 1 : HD + 2, :] * scale_b
    accum = (mine_ref[:HD, :] * scale_a + theirs_ref[:HD, :] * scale_b) / total
    for s in range(2):
        for g in range(GROUPS):
            start = (s * GROUPS + g) * SPAN
            out_ref[s * SPAN : (s + 1) * SPAN, g * HD : (g + 1) * HD] = accum[
                :, start : start + SPAN
            ].T.astype(bf16)


def finish(mine, theirs):
    return pl.pallas_call(
        finish_kernel,
        out_shape=jax.ShapeDtypeStruct((ROWS, GROUPS * HD), bf16),
        in_specs=vmem(2),
        out_specs=pl.BlockSpec(memory_space=pltpu.VMEM),
        compiler_params=pltpu.CompilerParams(vmem_limit_bytes=VMEM_LIMIT),
        name="finish",
    )(mine, theirs)


def on_device(patches, vis_pos, span_of, text_rows, proj_weight, norm_gain, qkv_weight):
    place = lax.axis_index("ctx")
    table = lax.all_to_all(
        jnp.broadcast_to(span_of[:, None, :], (OWNERS, 1, 2)), "ctx", split_axis=0, concat_axis=0, tiled=True
    ).reshape(2 * OWNERS)
    order = block_order()
    weight = jnp.transpose(qkv_weight, (2, 0, 1, 3)).reshape(GROUPS + 2, HEAD_DEVS, COLS, HD)
    gain = norm_gain.reshape(HEAD_DEVS, 1, COLS)

    visual = jnp.dot(patches, proj_weight, preferred_element_type=f32).astype(bf16)
    visual_blocks = head_gather(visual)
    text_blocks = head_gather(text_rows)

    matches = table[None, :] == (vis_pos // SPAN)[:, None]
    entry = jnp.sum(jnp.where(matches, jnp.arange(2 * OWNERS, dtype=jnp.int32)[None, :], 0), axis=1)
    owner = entry // 2
    count = vis_pos.shape[0]
    before = jnp.arange(count)[None, :] < jnp.arange(count)[:, None]
    rank = jnp.sum((owner[:, None] == owner[None, :]) & before, axis=1, dtype=jnp.int32)
    slots = (owner * CAP + rank)[None, :]
    marks = (entry % 2 * SPAN + vis_pos % SPAN + 1).astype(bf16)
    marks = jnp.broadcast_to(marks[:, None], (count, HD))

    vis_cos, vis_sin = rotary_tables(vis_pos)
    my_spans = span_of.reshape(2)
    row_pos = (my_spans[:, None] * SPAN + jnp.arange(SPAN, dtype=jnp.int32)[None, :]).reshape(ROWS)
    text_cos, text_sin = rotary_tables(row_pos)

    mail = project_qkv(order, visual_blocks, weight, gain, vis_cos, vis_sin, slots, marks)
    mail = lax.all_to_all(
        mail.reshape(OWNERS, CAP, MAIL), "ctx", split_axis=0, concat_axis=0, tiled=True
    ).reshape(SLOTS, MAIL)
    text_qkv = project_qkv(order, text_blocks, weight, gain, text_cos, text_sin)
    queries, own = merge_rows(mail, text_qkv)

    forth, back = z_shift(1), z_shift(-1)
    own_blocks = [lax.ppermute(own, "ctx", forth), lax.ppermute(own, "ctx", back)]
    side_blocks = [lax.ppermute(own, "ctx", xhi_swap())]
    other_queries = lax.ppermute(queries, "ctx", core_swap())
    both = (queries, other_queries)
    where = jnp.stack([place // 16, place // 2 % Z, place % 2]).astype(jnp.int32)
    step = functools.partial(attend, table, where, both)

    def send_on(blocks, hop):
        moved = [lax.ppermute(blocks[0], "ctx", forth)]
        if hop < 4:
            moved.append(lax.ppermute(blocks[-1], "ctx", back))
        return moved

    states = step([own], [(0, 0)], None)
    for hop in range(1, 5):
        own_blocks, states = lax.optimization_barrier((own_blocks, states))
        own_next = send_on(own_blocks, hop + 1) if hop < 4 else None
        side_blocks, states = lax.optimization_barrier((side_blocks, states))
        side_next = send_on(side_blocks, hop)
        places = [(1, 0)] if hop == 1 else [(1, 1 - hop), (1, hop - 1)]
        states = step(side_blocks, places, states)
        if hop < 4:
            states = step(own_blocks, [(0, -hop), (0, hop)], states)
            own_blocks = own_next
        side_blocks = side_next
    states = step([own_blocks[0], side_blocks[0]], [(0, -4), (1, -4)], states)
    mine, others = states
    theirs = lax.ppermute(others, "ctx", core_swap())
    return finish(mine, theirs)


def solution(mesh):
    in_specs = (
        P("ctx", None),
        P("ctx"),
        P("ctx", None),
        P("ctx", "head"),
        P(None, "head"),
        P(),
        P(None, "head", None, None),
    )
    out_specs = P("ctx", "head")
    return jax.shard_map(
        on_device, mesh=mesh, in_specs=in_specs, out_specs=out_specs, check_vma=False
    )
```

```python
import functools
import math

import jax
import jax.numpy as jnp
from jax import lax
from jax.experimental import pallas as pl
from jax.experimental.pallas import tpu as pltpu
from jax.sharding import PartitionSpec as P

HEADS = 32
KVH = 8
HD = 128
GROUPS = HEADS // KVH
WIDE = (GROUPS + 2) * HD
SPAN = 128
ROWS = 2 * SPAN
OWNERS = 32
CAP = ROWS // OWNERS
SLOTS = OWNERS * CAP
Z = 8
Y = 4
HEAD_DEVS = 8
COLS = 512
MAIL = WIDE + HD
QCOLS = GROUPS * ROWS
STATE = HD + 8

rope_theta = 500000.0
norm_eps = 1e-05
masked_score = -1e30
EXP_SCALE = HD ** (-0.5) * math.log2(math.e)
VMEM_LIMIT = 16 * 1024 * 1024
ATTEND_LIMIT = 8 * 1024 * 1024

bf16 = jnp.bfloat16
f32 = jnp.float32


def ctx_perm(move):
    return [(i, move(i)) for i in range(OWNERS)]


def z_shift(step):
    return ctx_perm(lambda i: (i // 16) * 16 + ((i // 2 % Z + step) % Z) * 2 + i % 2)


def core_swap():
    return ctx_perm(lambda i: i ^ 1)


def xhi_swap():
    return ctx_perm(lambda i: i ^ 16)


def y_shift(step):
    return [(i, (i // 2 + step) % Y * 2 + i % 2) for i in range(HEAD_DEVS)]


def xlo_swap():
    return [(i, i ^ 1) for i in range(HEAD_DEVS)]


def rotary_tables(positions):
    frequency = rope_theta ** (-jnp.arange(0, HD, 2, dtype=f32) / HD)
    angles = positions.astype(f32)[:, None] * frequency[None, :]
    cosine, sine = jnp.cos(angles), jnp.sin(angles)
    return jnp.concatenate([cosine, cosine], axis=1), jnp.concatenate([-sine, sine], axis=1)


def gather_first(own):
    return [
        lax.ppermute(own, "head", xlo_swap()),
        lax.ppermute(own, "head", y_shift(1)),
        lax.ppermute(own, "head", y_shift(-1)),
    ]


def gather_second(side, down, up):
    return [
        lax.ppermute(down, "head", y_shift(1)),
        lax.ppermute(side, "head", y_shift(-1)),
        lax.ppermute(down, "head", xlo_swap()),
    ]


def gather_third(far, side_up, side_down):
    half = far.shape[0] // 2
    return [
        lax.ppermute(side_down[:half], "head", y_shift(1)),
        lax.ppermute(side_up[half:], "head", y_shift(-1)),
    ]


def block_order(place):
    y, x = place // 2, place % 2

    def at(step, flip):
        return (y + step + Y) % Y * 2 + (x + flip) % 2

    return [at(0, 0), at(0, 1), at(-1, 0), at(1, 0), at(2, 0), at(1, 1), at(-1, 1), at(2, 1)]


def qkv_kernel(rows, send, *refs):
    blocks = refs[:9]
    weight_ref, gain_ref, cos_ref, sin_ref = refs[9:13]
    held, sems = refs[-2:]
    half = rows // 2
    order = block_order(lax.axis_index("head"))
    copies = [
        pltpu.make_async_copy(weight_ref.at[:, order[k]], held.at[k], sems.at[k]) for k in range(8)
    ]
    for copy in copies:
        copy.start()

    def block(k):
        if k < 7:
            return blocks[k][...].astype(f32)
        return jnp.concatenate([blocks[7][...], blocks[8][...]], axis=0).astype(f32)

    squares = jnp.zeros((rows, COLS), f32)
    for k in range(8):
        wide = block(k)
        squares = squares + wide * wide
    total = jnp.sum(squares, axis=1, keepdims=True)
    inverse = lax.rsqrt(total * (1.0 / (8 * COLS)) + norm_eps)
    pairs = (GROUPS + 2) // 2
    projected = [jnp.zeros((rows, 2 * HD), f32) for pair in range(pairs)]
    for k in range(8):
        normed = (block(k) * inverse * gain_ref[order[k]]).astype(bf16)
        copies[k].wait()
        for pair in range(pairs):
            weight = jnp.concatenate([held[k, 2 * pair], held[k, 2 * pair + 1]], axis=1)
            projected[pair] = projected[pair] + jnp.dot(
                normed, weight, preferred_element_type=f32
            )
    cosine, sine = cos_ref[...], sin_ref[...]
    parts = []
    for j in range(GROUPS + 2):
        slab = projected[j // 2][:, j % 2 * HD : (j % 2 + 1) * HD]
        if j <= GROUPS:
            slab = slab * cosine + pltpu.roll(slab, HD // 2, 1) * sine
        parts.append(slab.astype(bf16))
    if not send:
        out_ref = refs[13]
        for j in range(GROUPS + 2):
            out_ref[:, j * HD : (j + 1) * HD] = parts[j]
        return
    slot_ref, mark_ref, out_ref = refs[13:16]
    places = lax.broadcasted_iota(jnp.int32, (SLOTS, rows), 0)
    pick = jnp.where(places == slot_ref[...], 1.0, 0.0).astype(bf16)
    parts.append(mark_ref[...])
    for j in range(GROUPS + 3):
        out_ref[:, j * HD : (j + 1) * HD] = jnp.dot(
            pick, parts[j], preferred_element_type=f32
        ).astype(bf16)


def vmem(count):
    return [pl.BlockSpec(memory_space=pltpu.VMEM)] * count


def project_qkv(blocks, weight, gain, cosine, sine, slots=None, marks=None):
    rows = blocks[0].shape[0]
    send = slots is not None
    extra = (slots, marks) if send else ()
    return pl.pallas_call(
        functools.partial(qkv_kernel, rows, send),
        out_shape=jax.ShapeDtypeStruct((SLOTS, MAIL) if send else (rows, WIDE), bf16),
        in_specs=vmem(9) + [pl.BlockSpec(memory_space=pl.ANY)] + vmem(3 + len(extra)),
        out_specs=pl.BlockSpec(memory_space=pltpu.VMEM),
        scratch_shapes=[
            pltpu.VMEM((HEAD_DEVS, GROUPS + 2, COLS, HD), bf16),
            pltpu.SemaphoreType.DMA((HEAD_DEVS,)),
        ],
        compiler_params=pltpu.CompilerParams(vmem_limit_bytes=VMEM_LIMIT),
        cost_estimate=pl.CostEstimate(
            flops=2 * rows * 8 * COLS * WIDE, bytes_accessed=8 * COLS * WIDE * 2 + rows * 8192, transcendentals=0
        ),
        name="norm_qkv",
    )(*blocks, weight, gain, cosine, sine, *extra)


def merge_kernel(mail_ref, text_ref, query_ref, kv_ref):
    mail = mail_ref[...]
    marks = mail[:, WIDE : WIDE + 1].astype(f32)
    rows = (lax.broadcasted_iota(jnp.int32, (SLOTS, ROWS), 1) + 1).astype(f32)
    place = jnp.where(marks == rows, 1.0, 0.0).astype(bf16)
    placed = lax.dot_general(place, mail, (((0,), (0,)), ((), ())), preferred_element_type=f32)
    visual = placed[:, WIDE:] > 0.5
    for j in range(GROUPS + 2):
        cols = slice(j * HD, (j + 1) * HD)
        slab = jnp.where(visual, placed[:, cols], text_ref[:, cols].astype(f32))
        if j == GROUPS:
            kv_ref[:ROWS, :] = slab.astype(bf16)
            continue
        for s in range(2):
            turned = slab[s * SPAN : (s + 1) * SPAN, :].T.astype(bf16)
            if j < GROUPS:
                start = (s * GROUPS + j) * SPAN
                query_ref[:, start : start + SPAN] = turned
            else:
                kv_ref[ROWS + s * SPAN : ROWS + (s + 1) * SPAN, :] = turned


def merge_rows(mail, text):
    return pl.pallas_call(
        merge_kernel,
        out_shape=(
            jax.ShapeDtypeStruct((HD, QCOLS), bf16),
            jax.ShapeDtypeStruct((2 * ROWS, HD), bf16),
        ),
        in_specs=vmem(2),
        out_specs=tuple(vmem(2)),
        compiler_params=pltpu.CompilerParams(vmem_limit_bytes=VMEM_LIMIT),
        cost_estimate=pl.CostEstimate(
            flops=2 * SLOTS * ROWS * MAIL, bytes_accessed=4 * ROWS * MAIL, transcendentals=0
        ),
        name="merge_rows",
    )(mail, text)


def attend_kernel(first, count, key_row, *refs):
    key_ref, span_ref = refs[:2]
    query_refs = refs[2:4]
    kv_refs = refs[4 : 4 + count]
    ins, outs = refs[4 + count : -2], refs[-2:]
    keys = jnp.concatenate([kv[:ROWS, :] for kv in kv_refs], axis=0)
    values = jnp.concatenate(
        [kv[ROWS + s * SPAN : ROWS + (s + 1) * SPAN, :] for kv in kv_refs for s in range(2)], axis=1
    )
    row = lax.broadcasted_iota(jnp.int32, (SPAN, SPAN), 0).astype(f32)
    lane = lax.broadcasted_iota(jnp.int32, (SPAN, SPAN), 1).astype(f32)
    for half in range(2):
        for tile in range(QCOLS // SPAN):
            cols = slice(tile * SPAN, (tile + 1) * SPAN)
            query_span = span_ref[half : half + 1, cols]
            score = jnp.dot(keys, query_refs[half][:, cols], preferred_element_type=f32)
            pieces = []
            for j in range(2 * count):
                key_span = key_ref[key_row + j : key_row + j + 1, :]
                if first:
                    allowed = key_span * SPAN + row <= query_span * SPAN + lane
                else:
                    allowed = key_span < query_span
                pieces.append(jnp.where(allowed, score[j * SPAN : (j + 1) * SPAN, :], masked_score))
            score = jnp.concatenate(pieces, axis=0)
            high = jnp.max(score, axis=0, keepdims=True)
            if first:
                new_top = high
            else:
                top = ins[half][HD : HD + 1, cols]
                new_top = jnp.maximum(top, high)
                shrink = jnp.exp2((top - new_top) * EXP_SCALE)
            terms = jnp.exp2((score - new_top) * EXP_SCALE)
            total = jnp.sum(terms, axis=0, keepdims=True)
            accum = jnp.dot(values, terms.astype(bf16), preferred_element_type=f32)
            if not first:
                total = total + ins[half][HD + 1 : HD + 2, cols] * shrink
                accum = accum + ins[half][:HD, cols] * shrink
            outs[half][:HD, cols] = accum
            outs[half][HD : HD + 1, cols] = new_top
            outs[half][HD + 1 : HD + 2, cols] = total
            outs[half][HD + 2 : STATE, cols] = jnp.zeros((STATE - HD - 2, SPAN), f32)


def attend(key_spans, query_spans, queries, blocks, key_row, states):
    first = states is None
    count = len(blocks)
    given = () if first else tuple(states)
    return pl.pallas_call(
        functools.partial(attend_kernel, first, count, key_row),
        out_shape=(jax.ShapeDtypeStruct((STATE, QCOLS), f32),) * 2,
        in_specs=vmem(4 + count + len(given)),
        out_specs=tuple(vmem(2)),
        compiler_params=pltpu.CompilerParams(vmem_limit_bytes=ATTEND_LIMIT),
        cost_estimate=pl.CostEstimate(
            flops=4 * count * ROWS * 2 * QCOLS * HD,
            bytes_accessed=count * 4 * ROWS * HD + 2 * STATE * QCOLS * 8,
            transcendentals=count * ROWS * 2 * QCOLS,
        ),
        name="attend",
    )(key_spans, query_spans, *queries, *blocks, *given)


def finish_kernel(mine_ref, theirs_ref, out_ref):
    top_a, top_b = mine_ref[HD : HD + 1, :], theirs_ref[HD : HD + 1, :]
    top = jnp.maximum(top_a, top_b)
    scale_a = jnp.exp2((top_a - top) * EXP_SCALE)
    scale_b = jnp.exp2((top_b - top) * EXP_SCALE)
    total = mine_ref[HD + 1 : HD + 2, :] * scale_a + theirs_ref[HD + 1 : HD + 2, :] * scale_b
    accum = (mine_ref[:HD, :] * scale_a + theirs_ref[:HD, :] * scale_b) / total
    for s in range(2):
        for g in range(GROUPS):
            start = (s * GROUPS + g) * SPAN
            out_ref[s * SPAN : (s + 1) * SPAN, g * HD : (g + 1) * HD] = accum[
                :, start : start + SPAN
            ].T.astype(bf16)


def finish(mine, theirs):
    return pl.pallas_call(
        finish_kernel,
        out_shape=jax.ShapeDtypeStruct((ROWS, GROUPS * HD), bf16),
        in_specs=vmem(2),
        out_specs=pl.BlockSpec(memory_space=pltpu.VMEM),
        compiler_params=pltpu.CompilerParams(vmem_limit_bytes=VMEM_LIMIT),
        name="finish",
    )(mine, theirs)


def on_device(patches, vis_pos, span_of, text_rows, proj_weight, norm_gain, qkv_weight):
    place = lax.axis_index("ctx")
    x_hi, z, core = place // 16, place // 2 % Z, place % 2
    weight = jnp.transpose(qkv_weight, (2, 0, 1, 3)).reshape(GROUPS + 2, HEAD_DEVS, COLS, HD)
    gain = norm_gain.reshape(HEAD_DEVS, 1, COLS)

    visual = jnp.dot(patches, proj_weight, preferred_element_type=f32).astype(bf16)
    vis_first = gather_first(visual)
    text_first = gather_first(text_rows)
    my_table, visual = lax.optimization_barrier((span_of, visual))
    table = lax.all_to_all(
        jnp.broadcast_to(my_table[:, None, :], (OWNERS, 1, 2)), "ctx", split_axis=0, concat_axis=0, tiled=True
    ).reshape(2 * OWNERS)
    vis_second = gather_second(*vis_first)
    text_second = gather_second(*text_first)
    table, vis_second = lax.optimization_barrier((table, vis_second))
    vis_third = gather_third(*vis_second)
    text_second, vis_third = lax.optimization_barrier((text_second, vis_third))
    text_third = gather_third(*text_second)

    entries = jnp.arange(2 * OWNERS, dtype=jnp.int32)
    matches = table[None, :] == (vis_pos // SPAN)[:, None]
    entry = jnp.sum(jnp.where(matches, entries[None, :], 0), axis=1)
    owner = entry // 2
    count = vis_pos.shape[0]
    before = jnp.arange(count)[None, :] < jnp.arange(count)[:, None]
    rank = jnp.sum((owner[:, None] == owner[None, :]) & before, axis=1, dtype=jnp.int32)
    slots = (owner * CAP + rank)[None, :]
    marks = (entry % 2 * SPAN + vis_pos % SPAN + 1).astype(bf16)
    marks = jnp.broadcast_to(marks[:, None], (count, HD))

    taken = [(0, 0), (1, 0)]
    for hop in range(1, 4):
        taken += [(flip, shift) for flip in range(2) for shift in (-hop, hop)]
    taken += [(0, -4), (1, -4)]
    sources = [(((x_hi + flip) % 2) * Z + (z + shift + Z) % Z) * 2 + core for flip, shift in taken]
    mine = place
    other = place + 1 - 2 * core
    wanted = jnp.stack([2 * source + s for source in [*sources, mine, other] for s in range(2)])
    spans = jnp.sum(jnp.where(wanted[:, None] == entries[None, :], table[None, :], 0), axis=1).astype(f32)
    key_spans = jnp.broadcast_to(spans[:OWNERS, None], (OWNERS, SPAN))
    query_spans = jnp.broadcast_to(
        spans[OWNERS:].reshape(2, 2, 1), (2, 2, GROUPS * SPAN)
    ).reshape(2, QCOLS)

    vis_cos, vis_sin = rotary_tables(vis_pos)
    row_pos = (span_of.reshape(2, 1) * SPAN + jnp.arange(SPAN, dtype=jnp.int32)[None, :]).reshape(ROWS)
    text_cos, text_sin = rotary_tables(row_pos)

    mail = project_qkv(
        [visual, *vis_first, *vis_second, *vis_third], weight, gain, vis_cos, vis_sin, slots, marks
    )
    mail = lax.all_to_all(
        mail.reshape(OWNERS, CAP, MAIL), "ctx", split_axis=0, concat_axis=0, tiled=True
    ).reshape(SLOTS, MAIL)
    text_qkv = project_qkv(
        [text_rows, *text_first, *text_second, *text_third], weight, gain, text_cos, text_sin
    )
    queries, own = merge_rows(mail, text_qkv)

    forth, back = z_shift(1), z_shift(-1)
    own_blocks = [lax.ppermute(own, "ctx", forth), lax.ppermute(own, "ctx", back)]
    side_blocks = [lax.ppermute(own, "ctx", xhi_swap())]
    other_queries = lax.ppermute(queries, "ctx", core_swap())
    step = functools.partial(attend, key_spans, query_spans, (queries, other_queries))

    def send_on(blocks, hop):
        moved = [lax.ppermute(blocks[0], "ctx", forth)]
        if hop < 4:
            moved.append(lax.ppermute(blocks[-1], "ctx", back))
        return moved

    states = step([own], 0, None)
    key_row = 2
    for hop in range(1, 5):
        own_blocks, states = lax.optimization_barrier((own_blocks, states))
        own_next = send_on(own_blocks, hop + 1) if hop < 4 else None
        side_blocks, states = lax.optimization_barrier((side_blocks, states))
        side_next = send_on(side_blocks, hop)
        states = step(side_blocks, key_row, states)
        key_row += 2 * len(side_blocks)
        if hop < 4:
            states = step(own_blocks, key_row, states)
            key_row += 2 * len(own_blocks)
            own_blocks = own_next
        side_blocks = side_next
    states = step([own_blocks[0], side_blocks[0]], key_row, states)
    kept, given = states
    theirs = lax.ppermute(given, "ctx", core_swap())
    return finish(kept, theirs)


def solution(mesh):
    in_specs = (
        P("ctx", None),
        P("ctx"),
        P("ctx", None),
        P("ctx", "head"),
        P(None, "head"),
        P(),
        P(None, "head", None, None),
    )
    out_specs = P("ctx", "head")
    return jax.shard_map(
        on_device, mesh=mesh, in_specs=in_specs, out_specs=out_specs, check_vma=False
    )
```

```python
import functools
import math

import jax
import jax.numpy as jnp
from jax import lax
from jax.experimental import pallas as pl
from jax.experimental.pallas import tpu as pltpu
from jax.sharding import PartitionSpec as P

HEADS = 32
KVH = 8
HD = 128
GROUPS = HEADS // KVH
WIDE = (GROUPS + 2) * HD
SPAN = 128
ROWS = 2 * SPAN
OWNERS = 32
CAP = ROWS // OWNERS
SLOTS = OWNERS * CAP
Z = 8
Y = 4
HEAD_DEVS = 8
COLS = 512
MAIL = WIDE + HD
QCOLS = GROUPS * ROWS
STATE = HD + 8

rope_theta = 500000.0
norm_eps = 1e-05
masked_score = -1e30
EXP_SCALE = HD ** (-0.5) * math.log2(math.e)
VMEM_LIMIT = 16 * 1024 * 1024
ATTEND_LIMIT = 8 * 1024 * 1024

bf16 = jnp.bfloat16
f32 = jnp.float32


def ctx_perm(move):
    return [(i, move(i)) for i in range(OWNERS)]


def z_move():
    return ctx_perm(lambda i: (i // 16) * 16 + ((i // 2 % Z + 1 - 2 * (i % 2)) % Z) * 2 + i % 2)


def core_swap():
    return ctx_perm(lambda i: i ^ 1)


def xhi_swap():
    return ctx_perm(lambda i: i ^ 16)


def y_shift(step):
    return [(i, (i // 2 + step) % Y * 2 + i % 2) for i in range(HEAD_DEVS)]


def xlo_swap():
    return [(i, i ^ 1) for i in range(HEAD_DEVS)]


def rotary_tables(positions):
    frequency = rope_theta ** (-jnp.arange(0, HD, 2, dtype=f32) / HD)
    angles = positions.astype(f32)[:, None] * frequency[None, :]
    cosine, sine = jnp.cos(angles), jnp.sin(angles)
    return jnp.concatenate([cosine, cosine], axis=1), jnp.concatenate([-sine, sine], axis=1)


def gather_first(own):
    return [
        lax.ppermute(own, "head", xlo_swap()),
        lax.ppermute(own, "head", y_shift(1)),
        lax.ppermute(own, "head", y_shift(-1)),
    ]


def gather_second(side, down, up):
    return [
        lax.ppermute(down, "head", y_shift(1)),
        lax.ppermute(side, "head", y_shift(-1)),
        lax.ppermute(down, "head", xlo_swap()),
    ]


def gather_third(top, low):
    return [lax.ppermute(top, "head", y_shift(1)), lax.ppermute(low, "head", y_shift(-1))]


def block_order(place):
    y, x = place // 2, place % 2

    def at(step, flip):
        return (y + step + Y) % Y * 2 + (x + flip) % 2

    return [at(0, 0), at(0, 1), at(-1, 0), at(1, 0), at(2, 0), at(1, 1), at(-1, 1), at(2, 1)]


def qkv_kernel(rows, count, *refs):
    blocks, refs = refs[:count], refs[count:]
    weight_ref, gain_ref, cos_ref, sin_ref = refs[:4]
    order = block_order(lax.axis_index("head")) if count > 1 else list(range(HEAD_DEVS))

    def block(k):
        if count == 1:
            return blocks[0][:, k * COLS : (k + 1) * COLS].astype(f32)
        if k < 7:
            return blocks[k][...].astype(f32)
        return jnp.concatenate([blocks[7][...], blocks[8][...]], axis=0).astype(f32)

    squares = jnp.zeros((rows, COLS), f32)
    for k in range(8):
        wide = block(k)
        squares = squares + wide * wide
    total = jnp.sum(squares, axis=1, keepdims=True)
    inverse = lax.rsqrt(total * (1.0 / (8 * COLS)) + norm_eps)
    pairs = (GROUPS + 2) // 2
    projected = [jnp.zeros((rows, 2 * HD), f32) for pair in range(pairs)]
    for k in range(8):
        normed = (block(k) * inverse * gain_ref[order[k]]).astype(bf16)
        for pair in range(pairs):
            weight = jnp.concatenate(
                [weight_ref[2 * pair, order[k]], weight_ref[2 * pair + 1, order[k]]], axis=1
            )
            projected[pair] = projected[pair] + jnp.dot(
                normed, weight, preferred_element_type=f32
            )
    cosine, sine = cos_ref[...], sin_ref[...]
    parts = []
    for j in range(GROUPS + 2):
        slab = projected[j // 2][:, j % 2 * HD : (j % 2 + 1) * HD]
        if j <= GROUPS:
            slab = slab * cosine + pltpu.roll(slab, HD // 2, 1) * sine
        parts.append(slab)
    query_ref, kv_ref = refs[4:6]
    for j in range(GROUPS + 2):
        if j == GROUPS:
            kv_ref[:ROWS, :] = parts[j].astype(bf16)
            continue
        for s in range(2):
            turned = parts[j][s * SPAN : (s + 1) * SPAN, :].T.astype(bf16)
            if j < GROUPS:
                start = (s * GROUPS + j) * SPAN
                query_ref[:, start : start + SPAN] = turned
            else:
                kv_ref[ROWS + s * SPAN : ROWS + (s + 1) * SPAN, :] = turned


def vmem(count):
    return [pl.BlockSpec(memory_space=pltpu.VMEM)] * count


def load_kernel(weight_ref, out_ref, sems):
    copies = [
        pltpu.make_async_copy(weight_ref.at[j], out_ref.at[j], sems.at[j]) for j in range(GROUPS + 2)
    ]
    for copy in copies:
        copy.start()
    for copy in copies:
        copy.wait()


def load_weight(weight):
    return pl.pallas_call(
        load_kernel,
        out_shape=jax.ShapeDtypeStruct(weight.shape, bf16),
        in_specs=[pl.BlockSpec(memory_space=pltpu.HBM)],
        out_specs=pl.BlockSpec(memory_space=pltpu.VMEM),
        scratch_shapes=[pltpu.SemaphoreType.DMA((GROUPS + 2,))],
        compiler_params=pltpu.CompilerParams(vmem_limit_bytes=ATTEND_LIMIT),
        cost_estimate=pl.CostEstimate(flops=0, bytes_accessed=2 * weight.size * 2, transcendentals=0),
        name="load_weight",
    )(weight)


def project_qkv(blocks, weight, gain, cosine, sine):
    rows = blocks[0].shape[0]
    return pl.pallas_call(
        functools.partial(qkv_kernel, rows, len(blocks)),
        out_shape=(
            jax.ShapeDtypeStruct((HD, QCOLS), bf16),
            jax.ShapeDtypeStruct((2 * ROWS, HD), bf16),
        ),
        in_specs=vmem(len(blocks) + 4),
        out_specs=tuple(vmem(2)),
        compiler_params=pltpu.CompilerParams(vmem_limit_bytes=VMEM_LIMIT),
        cost_estimate=pl.CostEstimate(
            flops=2 * rows * 8 * COLS * WIDE, bytes_accessed=8 * COLS * WIDE * 2 + rows * 8192, transcendentals=0
        ),
        name="norm_qkv",
    )(*blocks, weight, gain, cosine, sine)


def route_kernel(rows_ref, slot_ref, mark_ref, out_ref):
    count = rows_ref.shape[0]
    places = lax.broadcasted_iota(jnp.int32, (SLOTS, count), 0)
    pick = jnp.where(places == slot_ref[...], 1.0, 0.0).astype(bf16)
    out_ref[:, :COLS] = jnp.dot(pick, rows_ref[...], preferred_element_type=f32).astype(bf16)
    out_ref[:, COLS:] = jnp.dot(pick, mark_ref[...], preferred_element_type=f32).astype(bf16)


def place_kernel(mail_ref, text_ref, out_ref):
    mail = mail_ref[...]
    marks = mail[:, COLS : COLS + 1].astype(f32)
    rows = (lax.broadcasted_iota(jnp.int32, (SLOTS, ROWS), 1) + 1).astype(f32)
    place = jnp.where(marks == rows, 1.0, 0.0).astype(bf16)
    placed = lax.dot_general(place, mail, (((0,), (0,)), ((), ())), preferred_element_type=f32)
    visual = placed[:, COLS:] > 0.5
    for j in range(COLS // HD):
        cols = slice(j * HD, (j + 1) * HD)
        out_ref[:, cols] = jnp.where(visual, placed[:, cols], text_ref[:, cols].astype(f32)).astype(bf16)


def whole(kernel, shape, name, *args):
    return pl.pallas_call(
        kernel,
        out_shape=jax.ShapeDtypeStruct(shape, bf16),
        in_specs=vmem(len(args)),
        out_specs=pl.BlockSpec(memory_space=pltpu.VMEM),
        compiler_params=pltpu.CompilerParams(vmem_limit_bytes=ATTEND_LIMIT),
        cost_estimate=pl.CostEstimate(flops=2 * SLOTS * ROWS * COLS, bytes_accessed=4 * ROWS * COLS, transcendentals=0),
        name=name,
    )(*args)


def attend_kernel(first, given, key_row, *refs):
    key_ref, span_ref = refs[:2]
    query_refs = refs[2:4]
    kv_refs = refs[4 : 4 + given]
    ins, outs = refs[4 + given : -2], refs[-2:]
    parts = [(kv, start) for kv in kv_refs for start in range(0, kv.shape[0], 2 * ROWS)]
    keys = jnp.concatenate([kv[start : start + ROWS, :] for kv, start in parts], axis=0)
    values = jnp.concatenate(
        [kv[start + ROWS + s * SPAN : start + ROWS + (s + 1) * SPAN, :] for kv, start in parts for s in range(2)],
        axis=1,
    )
    count = len(parts)
    row = lax.broadcasted_iota(jnp.int32, (SPAN, SPAN), 0).astype(f32)
    lane = lax.broadcasted_iota(jnp.int32, (SPAN, SPAN), 1).astype(f32)
    for half in range(2):
        for tile in range(QCOLS // SPAN):
            cols = slice(tile * SPAN, (tile + 1) * SPAN)
            query_span = span_ref[half : half + 1, cols]
            score = jnp.dot(keys, query_refs[half][:, cols], preferred_element_type=f32)
            pieces = []
            for j in range(2 * count):
                key_span = key_ref[key_row + j : key_row + j + 1, :]
                if first:
                    allowed = key_span * SPAN + row <= query_span * SPAN + lane
                else:
                    allowed = key_span < query_span
                pieces.append(jnp.where(allowed, score[j * SPAN : (j + 1) * SPAN, :], masked_score))
            score = jnp.concatenate(pieces, axis=0)
            high = jnp.max(score, axis=0, keepdims=True)
            if first:
                new_top = high
            else:
                top = ins[half][HD : HD + 1, cols]
                new_top = jnp.maximum(top, high)
                shrink = jnp.exp2((top - new_top) * EXP_SCALE)
            terms = jnp.exp2((score - new_top) * EXP_SCALE)
            total = jnp.sum(terms, axis=0, keepdims=True)
            accum = jnp.dot(values, terms.astype(bf16), preferred_element_type=f32)
            if not first:
                total = total + ins[half][HD + 1 : HD + 2, cols] * shrink
                accum = accum + ins[half][:HD, cols] * shrink
            outs[half][:HD, cols] = accum
            outs[half][HD : HD + 1, cols] = new_top
            outs[half][HD + 1 : HD + 2, cols] = total
            outs[half][HD + 2 : STATE, cols] = jnp.zeros((STATE - HD - 2, SPAN), f32)


def attend(key_spans, query_spans, queries, blocks, key_row, states):
    first = states is None
    count = len(blocks)
    given = () if first else tuple(states)
    return pl.pallas_call(
        functools.partial(attend_kernel, first, count, key_row),
        out_shape=(jax.ShapeDtypeStruct((STATE, QCOLS), f32),) * 2,
        in_specs=vmem(4 + count + len(given)),
        out_specs=tuple(vmem(2)),
        compiler_params=pltpu.CompilerParams(vmem_limit_bytes=ATTEND_LIMIT),
        cost_estimate=pl.CostEstimate(
            flops=4 * count * ROWS * 2 * QCOLS * HD,
            bytes_accessed=count * 4 * ROWS * HD + 2 * STATE * QCOLS * 8,
            transcendentals=count * ROWS * 2 * QCOLS,
        ),
        name="attend",
    )(key_spans, query_spans, *queries, *blocks, *given)


def finish_kernel(mine_ref, theirs_ref, out_ref):
    top_a, top_b = mine_ref[HD : HD + 1, :], theirs_ref[HD : HD + 1, :]
    top = jnp.maximum(top_a, top_b)
    scale_a = jnp.exp2((top_a - top) * EXP_SCALE)
    scale_b = jnp.exp2((top_b - top) * EXP_SCALE)
    total = mine_ref[HD + 1 : HD + 2, :] * scale_a + theirs_ref[HD + 1 : HD + 2, :] * scale_b
    accum = (mine_ref[:HD, :] * scale_a + theirs_ref[:HD, :] * scale_b) / total
    for s in range(2):
        for g in range(GROUPS):
            start = (s * GROUPS + g) * SPAN
            out_ref[s * SPAN : (s + 1) * SPAN, g * HD : (g + 1) * HD] = accum[
                :, start : start + SPAN
            ].T.astype(bf16)


def finish(mine, theirs):
    return pl.pallas_call(
        finish_kernel,
        out_shape=jax.ShapeDtypeStruct((ROWS, GROUPS * HD), bf16),
        in_specs=vmem(2),
        out_specs=pl.BlockSpec(memory_space=pltpu.VMEM),
        compiler_params=pltpu.CompilerParams(vmem_limit_bytes=VMEM_LIMIT),
        name="finish",
    )(mine, theirs)


def on_device(patches, vis_pos, span_of, text_rows, proj_weight, norm_gain, qkv_weight):
    place = lax.axis_index("ctx")
    x_hi, z, core = place // 16, place // 2 % Z, place % 2
    weight = jnp.transpose(qkv_weight, (2, 0, 1, 3)).reshape(GROUPS + 2, HEAD_DEVS, COLS, HD)
    gain = norm_gain.reshape(HEAD_DEVS, 1, COLS)

    table = lax.all_to_all(
        jnp.broadcast_to(span_of[:, None, :], (OWNERS, 1, 2)), "ctx", split_axis=0, concat_axis=0, tiled=True
    ).reshape(2 * OWNERS)
    visual = jnp.dot(patches, proj_weight, preferred_element_type=f32).astype(bf16)

    entries = jnp.arange(2 * OWNERS, dtype=jnp.int32)
    matches = table[None, :] == (vis_pos // SPAN)[:, None]
    entry = jnp.sum(jnp.where(matches, entries[None, :], 0), axis=1)
    owner = entry // 2
    count = vis_pos.shape[0]
    before = jnp.arange(count)[None, :] < jnp.arange(count)[:, None]
    rank = jnp.sum((owner[:, None] == owner[None, :]) & before, axis=1, dtype=jnp.int32)
    slots = (owner * CAP + rank)[None, :]
    marks = (entry % 2 * SPAN + vis_pos % SPAN + 1).astype(bf16)
    marks = jnp.broadcast_to(marks[:, None], (count, HD))

    taken = [(0, 0, 0), (0, 1, 0), (0, 1, 1), (1, 0, 0)]
    for hop in range(1, 3):
        taken += [(0, hop + 1, 0), (0, hop + 1, 1), (1, hop, 0), (1, hop, 1)]
    taken += [(1, 3, 0), (1, 3, 1), (0, 4, 0), (1, 4, 0)]
    back = 2 * core - 1
    sources = [
        (((x_hi + flip) % 2) * Z + (z + back * hop + Z) % Z) * 2 + (core + turn) % 2 for flip, hop, turn in taken
    ]
    mine = place
    other = place + 1 - 2 * core
    wanted = jnp.stack([2 * source + s for source in [*sources, mine, other] for s in range(2)])
    spans = jnp.sum(jnp.where(wanted[:, None] == entries[None, :], table[None, :], 0), axis=1).astype(f32)
    key_spans = jnp.broadcast_to(spans[:OWNERS, None], (OWNERS, SPAN))
    query_spans = jnp.broadcast_to(
        spans[OWNERS:].reshape(2, 2, 1), (2, 2, GROUPS * SPAN)
    ).reshape(2, QCOLS)

    row_pos = (span_of.reshape(2, 1) * SPAN + jnp.arange(SPAN, dtype=jnp.int32)[None, :]).reshape(ROWS)
    cosine, sine = rotary_tables(row_pos)

    mail = whole(route_kernel, (SLOTS, COLS + HD), "route_rows", visual, slots, marks)
    mail = lax.all_to_all(
        mail.reshape(OWNERS, CAP, COLS + HD), "ctx", split_axis=0, concat_axis=0, tiled=True
    ).reshape(SLOTS, COLS + HD)
    sequence = whole(place_kernel, (ROWS, COLS), "place_rows", mail, text_rows)
    first = lax.optimization_barrier(gather_first(sequence))
    second = lax.optimization_barrier(gather_second(*first))
    halves = (second[2][:SPAN], second[1][SPAN:])
    weight, gain, cosine, sine, halves = lax.optimization_barrier((weight, gain, cosine, sine, halves))
    third = gather_third(*halves)
    queries, own = project_qkv(
        [sequence, *first, *second, *third], load_weight(weight), gain, cosine, sine
    )

    side = lax.ppermute(own, "ctx", xhi_swap())
    stream = jnp.concatenate([own, lax.ppermute(own, "ctx", core_swap())], axis=0)
    stream, queries = lax.optimization_barrier((stream, queries))
    moved = lax.ppermute(stream, "ctx", z_move())
    other_queries = lax.ppermute(queries, "ctx", core_swap())
    step = functools.partial(attend, key_spans, query_spans, (queries, other_queries))
    states = step([own], 0, None)
    side, unused = lax.optimization_barrier((side, moved))
    side_stream = jnp.concatenate([side, lax.ppermute(side, "ctx", core_swap())], axis=0)
    side_held, side_moved = side, lax.ppermute(side_stream, "ctx", z_move())
    key_row = 2
    for hop in range(1, 4):
        size = 4 * ROWS if hop < 3 else 2 * ROWS
        moved, states = lax.optimization_barrier((moved, states))
        moved_next = lax.ppermute(moved[:size], "ctx", z_move())
        states = step([moved], key_row, states)
        key_row += 4
        states = step([side_held], key_row, states)
        key_row += 2 if hop == 1 else 4
        side_moved, states = lax.optimization_barrier((side_moved, states))
        side_next = lax.ppermute(side_moved[:size], "ctx", z_move())
        moved, side_held, side_moved = moved_next, side_moved, side_next
    states = step([side_held], key_row, states)
    states = step([moved, side_moved], key_row + 4, states)
    kept, given = states
    theirs = lax.ppermute(given, "ctx", core_swap())
    return finish(kept, theirs)


def solution(mesh):
    in_specs = (
        P("ctx", None),
        P("ctx"),
        P("ctx", None),
        P("ctx", "head"),
        P(None, "head"),
        P(),
        P(None, "head", None, None),
    )
    out_specs = P("ctx", "head")
    return jax.shard_map(
        on_device, mesh=mesh, in_specs=in_specs, out_specs=out_specs, check_vma=False
    )
```

```python
import functools
import math

import jax
import jax.numpy as jnp
from jax import lax
from jax.experimental import pallas as pl
from jax.experimental.pallas import tpu as pltpu
from jax.sharding import PartitionSpec as P

HEADS = 32
KVH = 8
HD = 128
GROUPS = HEADS // KVH
WIDE = (GROUPS + 2) * HD
SPAN = 128
ROWS = 2 * SPAN
OWNERS = 32
CAP = ROWS // OWNERS
SLOTS = OWNERS * CAP
Z = 8
Y = 4
HEAD_DEVS = 8
COLS = 512
MAIL = WIDE + HD
QCOLS = GROUPS * ROWS
STATE = HD + 8

MESSAGES = [(0, 1), (0, 2), (1, 1), (0, 3), (1, 2), (1, 3)]
GO_AFTER = {(0, 1): 0, (1, 1): 1, (0, 2): 1, (0, 3): 2, (1, 2): 3, (1, 3): 4}

rope_theta = 500000.0
norm_eps = 1e-05
masked_score = -1e30
EXP_SCALE = HD ** (-0.5) * math.log2(math.e)
VMEM_LIMIT = 16 * 1024 * 1024
ATTEND_LIMIT = 8 * 1024 * 1024

bf16 = jnp.bfloat16
f32 = jnp.float32


def ctx_perm(move):
    return [(i, move(i)) for i in range(OWNERS)]


def z_move():
    return ctx_perm(lambda i: (i // 16) * 16 + ((i // 2 % Z + 1 - 2 * (i % 2)) % Z) * 2 + i % 2)


def z_cross():
    return [(i, j ^ 16) for i, j in z_move()]


def core_swap():
    return ctx_perm(lambda i: i ^ 1)


def xhi_swap():
    return ctx_perm(lambda i: i ^ 16)


def y_shift(step):
    return [(i, (i // 2 + step) % Y * 2 + i % 2) for i in range(HEAD_DEVS)]


def xlo_swap():
    return [(i, i ^ 1) for i in range(HEAD_DEVS)]


def rotary_tables(positions):
    frequency = rope_theta ** (-jnp.arange(0, HD, 2, dtype=f32) / HD)
    angles = positions.astype(f32)[:, None] * frequency[None, :]
    cosine, sine = jnp.cos(angles), jnp.sin(angles)
    return jnp.concatenate([cosine, cosine], axis=1), jnp.concatenate([-sine, sine], axis=1)


def gather_first(own):
    return [
        lax.ppermute(own, "head", xlo_swap()),
        lax.ppermute(own, "head", y_shift(1)),
        lax.ppermute(own, "head", y_shift(-1)),
    ]


def gather_second(side, down, up):
    return [
        lax.ppermute(down, "head", y_shift(1)),
        lax.ppermute(side, "head", y_shift(-1)),
        lax.ppermute(down, "head", xlo_swap()),
    ]


def gather_third(top, low):
    return [lax.ppermute(top, "head", y_shift(1)), lax.ppermute(low, "head", y_shift(-1))]


def block_order(place):
    y, x = place // 2, place % 2

    def at(step, flip):
        return (y + step + Y) % Y * 2 + (x + flip) % 2

    return [at(0, 0), at(0, 1), at(-1, 0), at(1, 0), at(2, 0), at(1, 1), at(-1, 1), at(2, 1)]


def qkv_kernel(rows, count, *refs):
    blocks, refs = refs[:count], refs[count:]
    weight_ref, gain_ref, cos_ref, sin_ref = refs[:4]
    order = block_order(lax.axis_index("head")) if count > 1 else list(range(HEAD_DEVS))

    def block(k):
        if count == 1:
            return blocks[0][:, k * COLS : (k + 1) * COLS].astype(f32)
        if k < 7:
            return blocks[k][...].astype(f32)
        return jnp.concatenate([blocks[7][...], blocks[8][...]], axis=0).astype(f32)

    squares = jnp.zeros((rows, COLS), f32)
    for k in range(8):
        wide = block(k)
        squares = squares + wide * wide
    total = jnp.sum(squares, axis=1, keepdims=True)
    inverse = lax.rsqrt(total * (1.0 / (8 * COLS)) + norm_eps)
    pairs = (GROUPS + 2) // 2
    projected = [jnp.zeros((rows, 2 * HD), f32) for pair in range(pairs)]
    for k in range(8):
        normed = (block(k) * inverse * gain_ref[order[k]]).astype(bf16)
        for pair in range(pairs):
            weight = jnp.concatenate(
                [weight_ref[2 * pair, order[k]], weight_ref[2 * pair + 1, order[k]]], axis=1
            )
            projected[pair] = projected[pair] + jnp.dot(
                normed, weight, preferred_element_type=f32
            )
    cosine, sine = cos_ref[...], sin_ref[...]
    parts = []
    for j in range(GROUPS + 2):
        slab = projected[j // 2][:, j % 2 * HD : (j % 2 + 1) * HD]
        if j <= GROUPS:
            slab = slab * cosine + pltpu.roll(slab, HD // 2, 1) * sine
        parts.append(slab)
    query_ref, kv_ref = refs[4:6]
    for j in range(GROUPS + 2):
        if j == GROUPS:
            kv_ref[:ROWS, :] = parts[j].astype(bf16)
            continue
        for s in range(2):
            turned = parts[j][s * SPAN : (s + 1) * SPAN, :].T.astype(bf16)
            if j < GROUPS:
                start = (s * GROUPS + j) * SPAN
                query_ref[:, start : start + SPAN] = turned
            else:
                kv_ref[ROWS + s * SPAN : ROWS + (s + 1) * SPAN, :] = turned


def vmem(count):
    return [pl.BlockSpec(memory_space=pltpu.VMEM)] * count


def load_kernel(weight_ref, out_ref, sems):
    copies = [
        pltpu.make_async_copy(weight_ref.at[j], out_ref.at[j], sems.at[j]) for j in range(GROUPS + 2)
    ]
    for copy in copies:
        copy.start()
    for copy in copies:
        copy.wait()


def load_weight(weight):
    return pl.pallas_call(
        load_kernel,
        out_shape=jax.ShapeDtypeStruct(weight.shape, bf16),
        in_specs=[pl.BlockSpec(memory_space=pltpu.HBM)],
        out_specs=pl.BlockSpec(memory_space=pltpu.VMEM),
        scratch_shapes=[pltpu.SemaphoreType.DMA((GROUPS + 2,))],
        compiler_params=pltpu.CompilerParams(vmem_limit_bytes=ATTEND_LIMIT),
        cost_estimate=pl.CostEstimate(flops=0, bytes_accessed=2 * weight.size * 2, transcendentals=0),
        name="load_weight",
    )(weight)


def project_qkv(blocks, weight, gain, cosine, sine):
    rows = blocks[0].shape[0]
    return pl.pallas_call(
        functools.partial(qkv_kernel, rows, len(blocks)),
        out_shape=(
            jax.ShapeDtypeStruct((HD, QCOLS), bf16),
            jax.ShapeDtypeStruct((2 * ROWS, HD), bf16),
        ),
        in_specs=vmem(len(blocks) + 4),
        out_specs=tuple(vmem(2)),
        compiler_params=pltpu.CompilerParams(vmem_limit_bytes=VMEM_LIMIT),
        cost_estimate=pl.CostEstimate(
            flops=2 * rows * 8 * COLS * WIDE, bytes_accessed=8 * COLS * WIDE * 2 + rows * 8192, transcendentals=0
        ),
        name="norm_qkv",
    )(*blocks, weight, gain, cosine, sine)


def entry_kernel(span_ref, out_ref):
    lane = lax.broadcasted_iota(jnp.int32, (OWNERS, HD), 1) - 2 * lax.axis_index("ctx")
    first = jnp.broadcast_to(span_ref[:, :1], (OWNERS, HD))
    second = jnp.broadcast_to(span_ref[:, 1:], (OWNERS, HD))
    out_ref[...] = jnp.where(lane == 0, first, jnp.where(lane == 1, second, 0))


def route_kernel(rows_ref, pos_ref, table_ref, out_ref):
    count = rows_ref.shape[0]
    lane = lax.broadcasted_iota(jnp.int32, (count, HD), 1)
    table = jnp.sum(table_ref[...].astype(f32), axis=0, keepdims=True)
    matches = (pos_ref[...] // SPAN).astype(f32) == jnp.where(lane < 2 * OWNERS, table, -1.0)
    entry = jnp.sum(jnp.where(matches, lane.astype(f32), 0.0), axis=1, keepdims=True).astype(jnp.int32)
    owner = entry // 2
    same = jnp.where(lane // 2 == owner, 1.0, 0.0).astype(bf16)
    square = (count, count)
    before = lax.broadcasted_iota(jnp.int32, square, 1) < lax.broadcasted_iota(jnp.int32, square, 0)
    ranks = jnp.dot(jnp.where(before, 1.0, 0.0).astype(bf16), same, preferred_element_type=f32)
    rank = jnp.sum(jnp.where(matches, ranks, 0.0), axis=1, keepdims=True).astype(jnp.int32)
    slot = owner * CAP + rank
    pick = jnp.where(lax.broadcasted_iota(jnp.int32, (count, SLOTS), 1) == slot, 1.0, 0.0).astype(bf16)
    mark = (entry % 2 * SPAN + pos_ref[...] % SPAN + 1).astype(f32)
    marks = jnp.broadcast_to(mark, (count, HD)).astype(bf16)
    across = (((0,), (0,)), ((), ()))
    out_ref[:, :COLS] = lax.dot_general(pick, rows_ref[...], across, preferred_element_type=f32).astype(bf16)
    out_ref[:, COLS:] = lax.dot_general(pick, marks, across, preferred_element_type=f32).astype(bf16)


def place_kernel(mail_ref, text_ref, out_ref):
    mail = mail_ref[...]
    marks = mail[:, COLS : COLS + 1].astype(f32)
    rows = (lax.broadcasted_iota(jnp.int32, (SLOTS, ROWS), 1) + 1).astype(f32)
    place = jnp.where(marks == rows, 1.0, 0.0).astype(bf16)
    placed = lax.dot_general(place, mail, (((0,), (0,)), ((), ())), preferred_element_type=f32)
    visual = placed[:, COLS:] > 0.5
    for j in range(COLS // HD):
        cols = slice(j * HD, (j + 1) * HD)
        out_ref[:, cols] = jnp.where(visual, placed[:, cols], text_ref[:, cols].astype(f32)).astype(bf16)


def whole(kernel, shape, name, *args):
    return pl.pallas_call(
        kernel,
        out_shape=jax.ShapeDtypeStruct(shape, bf16),
        in_specs=vmem(len(args)),
        out_specs=pl.BlockSpec(memory_space=pltpu.VMEM),
        compiler_params=pltpu.CompilerParams(vmem_limit_bytes=ATTEND_LIMIT),
        cost_estimate=pl.CostEstimate(flops=2 * SLOTS * ROWS * COLS, bytes_accessed=4 * ROWS * COLS, transcendentals=0),
        name=name,
    )(*args)


def attend_kernel(first, given, key_row, halves, *refs):
    key_ref, span_ref = refs[:2]
    query_refs = refs[2:4]
    kv_refs = refs[4 : 4 + given]
    ins, outs = refs[4 + given : -len(halves)], refs[-len(halves) :]
    parts = [(kv, start) for kv in kv_refs for start in range(0, kv.shape[0], 2 * ROWS)]
    keys = jnp.concatenate([kv[start : start + ROWS, :] for kv, start in parts], axis=0)
    values = jnp.concatenate(
        [kv[start + ROWS + s * SPAN : start + ROWS + (s + 1) * SPAN, :] for kv, start in parts for s in range(2)],
        axis=1,
    )
    count = 2 * len(parts)
    row = lax.broadcasted_iota(jnp.int32, (SPAN, SPAN), 0).astype(f32)
    lane = lax.broadcasted_iota(jnp.int32, (SPAN, SPAN), 1).astype(f32)
    for place, half in enumerate(halves):
        for tile in range(QCOLS // SPAN):
            cols = slice(tile * SPAN, (tile + 1) * SPAN)
            query_span = span_ref[half : half + 1, cols]
            score = jnp.dot(keys, query_refs[half][:, cols], preferred_element_type=f32)
            pieces = [score[j * SPAN : (j + 1) * SPAN, :] for j in range(count)]
            key_spans = [key_ref[key_row + j : key_row + j + 1, :] for j in range(count)]
            if first:
                pieces = [
                    jnp.where(span * SPAN + row <= query_span * SPAN + lane, piece, masked_score)
                    for span, piece in zip(key_spans, pieces)
                ]
                new_top = functools.reduce(
                    jnp.maximum, [jnp.max(piece, axis=0, keepdims=True) for piece in pieces]
                )
                shifts = [new_top] * count
            else:
                top = ins[place][HD : HD + 1, cols]
                allowed = [span < query_span for span in key_spans]
                highs = [
                    jnp.where(ok, jnp.max(piece, axis=0, keepdims=True), masked_score)
                    for ok, piece in zip(allowed, pieces)
                ]
                new_top = functools.reduce(jnp.maximum, highs, top)
                shrink = jnp.exp2((top - new_top) * EXP_SCALE)
                shifts = [jnp.where(ok, new_top, -masked_score) for ok in allowed]
            terms = jnp.concatenate(
                [jnp.exp2((piece - shift) * EXP_SCALE) for piece, shift in zip(pieces, shifts)], axis=0
            )
            total = jnp.sum(terms, axis=0, keepdims=True)
            accum = jnp.dot(values, terms.astype(bf16), preferred_element_type=f32)
            if not first:
                total = total + ins[place][HD + 1 : HD + 2, cols] * shrink
                accum = accum + ins[place][:HD, cols] * shrink
            out = outs[place]
            out[:HD, cols] = accum
            out[HD : HD + 1, cols] = new_top
            out[HD + 1 : HD + 2, cols] = total
            out[HD + 2 : STATE, cols] = jnp.zeros((STATE - HD - 2, SPAN), f32)


def attend(key_spans, query_spans, queries, blocks, key_row, states, halves=(0, 1)):
    first = states is None
    given = () if first else tuple(states[half] for half in halves)
    return pl.pallas_call(
        functools.partial(attend_kernel, first, len(blocks), key_row, halves),
        out_shape=(jax.ShapeDtypeStruct((STATE, QCOLS), f32),) * len(halves),
        in_specs=vmem(4 + len(blocks) + len(given)),
        out_specs=tuple(vmem(len(halves))),
        compiler_params=pltpu.CompilerParams(vmem_limit_bytes=ATTEND_LIMIT),
        cost_estimate=pl.CostEstimate(
            flops=16 * ROWS * len(halves) * QCOLS * HD,
            bytes_accessed=8 * ROWS * HD + 2 * STATE * QCOLS * 8,
            transcendentals=2 * ROWS * len(halves) * QCOLS,
        ),
        name="attend",
    )(key_spans, query_spans, *queries, *blocks, *given)


def finish_kernel(mine_ref, theirs_ref, out_ref):
    top_a, top_b = mine_ref[HD : HD + 1, :], theirs_ref[HD : HD + 1, :]
    top = jnp.maximum(top_a, top_b)
    scale_a = jnp.exp2((top_a - top) * EXP_SCALE)
    scale_b = jnp.exp2((top_b - top) * EXP_SCALE)
    total = mine_ref[HD + 1 : HD + 2, :] * scale_a + theirs_ref[HD + 1 : HD + 2, :] * scale_b
    accum = (mine_ref[:HD, :] * scale_a + theirs_ref[:HD, :] * scale_b) / total
    for s in range(2):
        for g in range(GROUPS):
            start = (s * GROUPS + g) * SPAN
            out_ref[s * SPAN : (s + 1) * SPAN, g * HD : (g + 1) * HD] = accum[
                :, start : start + SPAN
            ].T.astype(bf16)


def finish(mine, theirs):
    return pl.pallas_call(
        finish_kernel,
        out_shape=jax.ShapeDtypeStruct((ROWS, GROUPS * HD), bf16),
        in_specs=vmem(2),
        out_specs=pl.BlockSpec(memory_space=pltpu.VMEM),
        compiler_params=pltpu.CompilerParams(vmem_limit_bytes=VMEM_LIMIT),
        name="finish",
    )(mine, theirs)


def send_on(block, before, size):
    block, unused = lax.optimization_barrier((block, before))
    return lax.ppermute(block[:size], "ctx", z_move())


def on_device(patches, vis_pos, span_of, text_rows, proj_weight, norm_gain, qkv_weight):
    place = lax.axis_index("ctx")
    x_hi, z, core = place // 16, place // 2 % Z, place % 2
    weight = jnp.transpose(qkv_weight, (2, 0, 1, 3)).reshape(GROUPS + 2, HEAD_DEVS, COLS, HD)
    gain = norm_gain.reshape(HEAD_DEVS, 1, COLS)

    lanes = jnp.arange(HD, dtype=jnp.int32)[None, :]
    my_rows = pl.pallas_call(
        entry_kernel,
        out_shape=jax.ShapeDtypeStruct((OWNERS, HD), jnp.int32),
        in_specs=vmem(1),
        out_specs=pl.BlockSpec(memory_space=pltpu.VMEM),
        name="my_entry",
    )(span_of)
    table_rows = lax.all_to_all(
        my_rows.reshape(OWNERS, 1, HD), "ctx", split_axis=0, concat_axis=0, tiled=True
    ).reshape(OWNERS, HD)
    visual = jnp.dot(patches, proj_weight, preferred_element_type=f32).astype(bf16)

    taken = [(0, 0, 0)]
    for flip, hop in MESSAGES:
        taken += [(flip, hop, 0), (flip, hop, 1)]
    taken += [(1, 0, 0), (0, 4, 0), (1, 4, 0)]
    back = 2 * core - 1
    sources = [
        (((x_hi + flip) % 2) * Z + (z + back * hop + Z) % Z) * 2 + (core + turn) % 2 for flip, hop, turn in taken
    ]
    mine = place
    other = place + 1 - 2 * core
    wanted = jnp.stack([2 * source + s for source in [*sources, mine, other] for s in range(2)])
    table = jnp.sum(table_rows, axis=0)[None, :]
    spans = jnp.sum(jnp.where(wanted[:, None] == lanes, table, 0), axis=1).astype(f32)
    key_spans = jnp.broadcast_to(spans[:OWNERS, None], (OWNERS, SPAN))
    query_spans = jnp.broadcast_to(
        spans[OWNERS:].reshape(2, 2, 1), (2, 2, GROUPS * SPAN)
    ).reshape(2, QCOLS)

    row_pos = (span_of.reshape(2, 1) * SPAN + jnp.arange(SPAN, dtype=jnp.int32)[None, :]).reshape(ROWS)
    cosine, sine = rotary_tables(row_pos)

    mail = whole(route_kernel, (SLOTS, COLS + HD), "route_rows", visual, vis_pos[:, None], table_rows)
    mail = lax.all_to_all(
        mail.reshape(OWNERS, CAP, COLS + HD), "ctx", split_axis=0, concat_axis=0, tiled=True
    ).reshape(SLOTS, COLS + HD)
    sequence = whole(place_kernel, (ROWS, COLS), "place_rows", mail, text_rows)
    first = lax.optimization_barrier(gather_first(sequence))
    second = lax.optimization_barrier(gather_second(*first))
    halves = (second[2][:SPAN], second[1][SPAN:])
    weight, gain, cosine, sine, halves = lax.optimization_barrier((weight, gain, cosine, sine, halves))
    third = gather_third(*halves)
    queries, own = project_qkv(
        [sequence, *first, *second, *third], load_weight(weight), gain, cosine, sine
    )

    stream = jnp.concatenate([own, lax.ppermute(own, "ctx", core_swap())], axis=0)
    stream, queries, own = lax.optimization_barrier((stream, queries, own))
    moved = lax.ppermute(stream, "ctx", z_move())
    crossed = lax.ppermute(stream, "ctx", z_cross())
    other_queries = lax.ppermute(queries, "ctx", core_swap())
    side = lax.ppermute(own, "ctx", xhi_swap())
    step = functools.partial(attend, key_spans, query_spans, (queries, other_queries))
    states = step([own], 0, None)
    key_row = 2
    history = [states]
    held = {(0, 1): moved, (1, 1): crossed}
    for message in MESSAGES:
        held_now = dict(held)
        for (line, hop), block in held_now.items():
            if GO_AFTER.get((line, hop)) == len(history) - 1:
                held[line, hop + 1] = send_on(block, states, 4 * ROWS if hop < 3 else 2 * ROWS)
        states = step([held[message]], key_row, states)
        key_row += 4
        history.append(states)
    states = step([side], key_row, states)
    key_row += 2
    moved, crossed = held[0, 4], held[1, 4]
    (given,) = step([moved, crossed], key_row, states, (1,))
    theirs = lax.ppermute(given, "ctx", core_swap())
    (kept,) = step([moved, crossed], key_row, states, (0,))
    return finish(kept, theirs)


def solution(mesh):
    in_specs = (
        P("ctx", None),
        P("ctx"),
        P("ctx", None),
        P("ctx", "head"),
        P(None, "head"),
        P(),
        P(None, "head", None, None),
    )
    out_specs = P("ctx", "head")
    return jax.shard_map(
        on_device, mesh=mesh, in_specs=in_specs, out_specs=out_specs, check_vma=False
    )
```

```python
import functools
import math

import jax
import jax.numpy as jnp
from jax import lax
from jax.experimental import pallas as pl
from jax.experimental.pallas import tpu as pltpu
from jax.sharding import PartitionSpec as P

HEADS = 32
KVH = 8
HD = 128
GROUPS = HEADS // KVH
WIDE = (GROUPS + 2) * HD
SPAN = 128
ROWS = 2 * SPAN
OWNERS = 32
CAP = ROWS // OWNERS
SLOTS = OWNERS * CAP
Z = 8
Y = 4
HEAD_DEVS = 8
COLS = 512
MAIL = WIDE + HD
QCOLS = GROUPS * ROWS
STATE = HD + 8

MESSAGES = [(0, 1), (0, 2), (1, 1), (0, 3), (1, 2), (1, 3)]
SENDS = [(0, 0, 1, 2), (1, 0, 2, 3), (1, 1, 1, 2), (1, 1, 1, 3), (2, 0, 3, 4), (3, 1, 2, 4)]

rope_theta = 500000.0
norm_eps = 1e-05
masked_score = -1e30
EXP_SCALE = HD ** (-0.5) * math.log2(math.e)
VMEM_LIMIT = 16 * 1024 * 1024
ATTEND_LIMIT = 8 * 1024 * 1024

bf16 = jnp.bfloat16
f32 = jnp.float32


def ctx_perm(move):
    return [(i, move(i)) for i in range(OWNERS)]


def z_move(steps=1):
    return ctx_perm(lambda i: (i // 16) * 16 + ((i // 2 % Z + steps * (1 - 2 * (i % 2))) % Z) * 2 + i % 2)


def z_cross():
    return [(i, j ^ 16) for i, j in z_move()]


def core_swap():
    return ctx_perm(lambda i: i ^ 1)


def xhi_swap():
    return ctx_perm(lambda i: i ^ 16)


def y_shift(step):
    return [(i, (i // 2 + step) % Y * 2 + i % 2) for i in range(HEAD_DEVS)]


def xlo_swap():
    return [(i, i ^ 1) for i in range(HEAD_DEVS)]


def rotary_tables(positions):
    frequency = rope_theta ** (-jnp.arange(0, HD, 2, dtype=f32) / HD)
    angles = positions.astype(f32)[:, None] * frequency[None, :]
    cosine, sine = jnp.cos(angles), jnp.sin(angles)
    return jnp.concatenate([cosine, cosine], axis=1), jnp.concatenate([-sine, sine], axis=1)


def gather_first(own):
    return [
        lax.ppermute(own, "head", xlo_swap()),
        lax.ppermute(own, "head", y_shift(1)),
        lax.ppermute(own, "head", y_shift(-1)),
    ]


def gather_second(side, down, up):
    return [
        lax.ppermute(down, "head", y_shift(1)),
        lax.ppermute(side, "head", y_shift(-1)),
        lax.ppermute(down, "head", xlo_swap()),
    ]


def gather_third(top, low):
    return [lax.ppermute(top, "head", y_shift(1)), lax.ppermute(low, "head", y_shift(-1))]


def block_order(place):
    y, x = place // 2, place % 2

    def at(step, flip):
        return (y + step + Y) % Y * 2 + (x + flip) % 2

    return [at(0, 0), at(0, 1), at(-1, 0), at(1, 0), at(2, 0), at(1, 1), at(-1, 1), at(2, 1)]


def qkv_kernel(rows, count, *refs):
    blocks, refs = refs[:count], refs[count:]
    weight_ref, gain_ref, cos_ref, sin_ref = refs[:4]
    order = block_order(lax.axis_index("head")) if count > 1 else list(range(HEAD_DEVS))

    def block(k):
        if count == 1:
            return blocks[0][:, k * COLS : (k + 1) * COLS].astype(f32)
        if k < 7:
            return blocks[k][...].astype(f32)
        return jnp.concatenate([blocks[7][...], blocks[8][...]], axis=0).astype(f32)

    squares = jnp.zeros((rows, COLS), f32)
    for k in range(8):
        wide = block(k)
        squares = squares + wide * wide
    total = jnp.sum(squares, axis=1, keepdims=True)
    inverse = lax.rsqrt(total * (1.0 / (8 * COLS)) + norm_eps)
    pairs = (GROUPS + 2) // 2
    projected = [jnp.zeros((rows, 2 * HD), f32) for pair in range(pairs)]
    for k in range(8):
        normed = (block(k) * inverse * gain_ref[order[k]]).astype(bf16)
        for pair in range(pairs):
            weight = jnp.concatenate(
                [weight_ref[2 * pair, order[k]], weight_ref[2 * pair + 1, order[k]]], axis=1
            )
            projected[pair] = projected[pair] + jnp.dot(
                normed, weight, preferred_element_type=f32
            )
    cosine, sine = cos_ref[...], sin_ref[...]
    parts = []
    for j in range(GROUPS + 2):
        slab = projected[j // 2][:, j % 2 * HD : (j % 2 + 1) * HD]
        if j <= GROUPS:
            slab = slab * cosine + pltpu.roll(slab, HD // 2, 1) * sine
        parts.append(slab)
    query_ref, kv_ref = refs[4:6]
    for j in range(GROUPS + 2):
        if j == GROUPS:
            kv_ref[:ROWS, :] = parts[j].astype(bf16)
            continue
        for s in range(2):
            turned = parts[j][s * SPAN : (s + 1) * SPAN, :].T.astype(bf16)
            if j < GROUPS:
                start = (s * GROUPS + j) * SPAN
                query_ref[:, start : start + SPAN] = turned
            else:
                kv_ref[ROWS + s * SPAN : ROWS + (s + 1) * SPAN, :] = turned


def vmem(count):
    return [pl.BlockSpec(memory_space=pltpu.VMEM)] * count


def load_kernel(weight_ref, out_ref, sems):
    copies = [
        pltpu.make_async_copy(weight_ref.at[j], out_ref.at[j], sems.at[j]) for j in range(GROUPS + 2)
    ]
    for copy in copies:
        copy.start()
    for copy in copies:
        copy.wait()


def load_weight(weight):
    return pl.pallas_call(
        load_kernel,
        out_shape=jax.ShapeDtypeStruct(weight.shape, bf16),
        in_specs=[pl.BlockSpec(memory_space=pltpu.HBM)],
        out_specs=pl.BlockSpec(memory_space=pltpu.VMEM),
        scratch_shapes=[pltpu.SemaphoreType.DMA((GROUPS + 2,))],
        compiler_params=pltpu.CompilerParams(vmem_limit_bytes=ATTEND_LIMIT),
        cost_estimate=pl.CostEstimate(flops=0, bytes_accessed=2 * weight.size * 2, transcendentals=0),
        name="load_weight",
    )(weight)


def project_qkv(blocks, weight, gain, cosine, sine):
    rows = blocks[0].shape[0]
    return pl.pallas_call(
        functools.partial(qkv_kernel, rows, len(blocks)),
        out_shape=(
            jax.ShapeDtypeStruct((HD, QCOLS), bf16),
            jax.ShapeDtypeStruct((2 * ROWS, HD), bf16),
        ),
        in_specs=vmem(len(blocks) + 4),
        out_specs=tuple(vmem(2)),
        compiler_params=pltpu.CompilerParams(vmem_limit_bytes=VMEM_LIMIT),
        cost_estimate=pl.CostEstimate(
            flops=2 * rows * 8 * COLS * WIDE, bytes_accessed=8 * COLS * WIDE * 2 + rows * 8192, transcendentals=0
        ),
        name="norm_qkv",
    )(*blocks, weight, gain, cosine, sine)


def entry_kernel(span_ref, out_ref):
    lane = lax.broadcasted_iota(jnp.int32, (OWNERS, HD), 1) - 2 * lax.axis_index("ctx")
    first = jnp.broadcast_to(span_ref[:, :1], (OWNERS, HD))
    second = jnp.broadcast_to(span_ref[:, 1:], (OWNERS, HD))
    out_ref[...] = jnp.where(lane == 0, first, jnp.where(lane == 1, second, 0))


def route_kernel(rows_ref, pos_ref, table_ref, out_ref):
    count = rows_ref.shape[0]
    lane = lax.broadcasted_iota(jnp.int32, (count, HD), 1)
    table = jnp.sum(table_ref[...].astype(f32), axis=0, keepdims=True)
    matches = (pos_ref[...] // SPAN).astype(f32) == jnp.where(lane < 2 * OWNERS, table, -1.0)
    entry = jnp.sum(jnp.where(matches, lane.astype(f32), 0.0), axis=1, keepdims=True).astype(jnp.int32)
    owner = entry // 2
    same = jnp.where(lane // 2 == owner, 1.0, 0.0).astype(bf16)
    square = (count, count)
    before = lax.broadcasted_iota(jnp.int32, square, 1) < lax.broadcasted_iota(jnp.int32, square, 0)
    ranks = jnp.dot(jnp.where(before, 1.0, 0.0).astype(bf16), same, preferred_element_type=f32)
    rank = jnp.sum(jnp.where(matches, ranks, 0.0), axis=1, keepdims=True).astype(jnp.int32)
    slot = owner * CAP + rank
    pick = jnp.where(lax.broadcasted_iota(jnp.int32, (count, SLOTS), 1) == slot, 1.0, 0.0).astype(bf16)
    mark = (entry % 2 * SPAN + pos_ref[...] % SPAN + 1).astype(f32)
    marks = jnp.broadcast_to(mark, (count, HD)).astype(bf16)
    across = (((0,), (0,)), ((), ()))
    out_ref[:, :COLS] = lax.dot_general(pick, rows_ref[...], across, preferred_element_type=f32).astype(bf16)
    out_ref[:, COLS:] = lax.dot_general(pick, marks, across, preferred_element_type=f32).astype(bf16)


def place_kernel(mail_ref, text_ref, out_ref):
    mail = mail_ref[...]
    marks = mail[:, COLS : COLS + 1].astype(f32)
    rows = (lax.broadcasted_iota(jnp.int32, (SLOTS, ROWS), 1) + 1).astype(f32)
    place = jnp.where(marks == rows, 1.0, 0.0).astype(bf16)
    placed = lax.dot_general(place, mail, (((0,), (0,)), ((), ())), preferred_element_type=f32)
    visual = placed[:, COLS:] > 0.5
    for j in range(COLS // HD):
        cols = slice(j * HD, (j + 1) * HD)
        out_ref[:, cols] = jnp.where(visual, placed[:, cols], text_ref[:, cols].astype(f32)).astype(bf16)


def whole(kernel, shape, name, *args):
    return pl.pallas_call(
        kernel,
        out_shape=jax.ShapeDtypeStruct(shape, bf16),
        in_specs=vmem(len(args)),
        out_specs=pl.BlockSpec(memory_space=pltpu.VMEM),
        compiler_params=pltpu.CompilerParams(vmem_limit_bytes=ATTEND_LIMIT),
        cost_estimate=pl.CostEstimate(flops=2 * SLOTS * ROWS * COLS, bytes_accessed=4 * ROWS * COLS, transcendentals=0),
        name=name,
    )(*args)


def attend_kernel(first, given, key_row, halves, *refs):
    key_ref, span_ref = refs[:2]
    query_refs = refs[2:4]
    kv_refs = refs[4 : 4 + given]
    ins, outs = refs[4 + given : -len(halves)], refs[-len(halves) :]
    parts = [(kv, start) for kv in kv_refs for start in range(0, kv.shape[0], 2 * ROWS)]
    keys = jnp.concatenate([kv[start : start + ROWS, :] for kv, start in parts], axis=0)
    values = jnp.concatenate(
        [kv[start + ROWS + s * SPAN : start + ROWS + (s + 1) * SPAN, :] for kv, start in parts for s in range(2)],
        axis=1,
    )
    count = 2 * len(parts)
    row = lax.broadcasted_iota(jnp.int32, (SPAN, SPAN), 0).astype(f32)
    lane = lax.broadcasted_iota(jnp.int32, (SPAN, SPAN), 1).astype(f32)
    for place, half in enumerate(halves):
        for tile in range(QCOLS // SPAN):
            cols = slice(tile * SPAN, (tile + 1) * SPAN)
            query_span = span_ref[half : half + 1, cols]
            score = jnp.dot(keys, query_refs[half][:, cols], preferred_element_type=f32)
            pieces = [score[j * SPAN : (j + 1) * SPAN, :] for j in range(count)]
            key_spans = [key_ref[key_row + j : key_row + j + 1, :] for j in range(count)]
            if first:
                pieces = [
                    jnp.where(span * SPAN + row <= query_span * SPAN + lane, piece, masked_score)
                    for span, piece in zip(key_spans, pieces)
                ]
                new_top = functools.reduce(
                    jnp.maximum, [jnp.max(piece, axis=0, keepdims=True) for piece in pieces]
                )
                shifts = [new_top] * count
            else:
                top = ins[place][HD : HD + 1, cols]
                allowed = [span < query_span for span in key_spans]
                highs = [
                    jnp.where(ok, jnp.max(piece, axis=0, keepdims=True), masked_score)
                    for ok, piece in zip(allowed, pieces)
                ]
                new_top = functools.reduce(jnp.maximum, highs, top)
                shrink = jnp.exp2((top - new_top) * EXP_SCALE)
                shifts = [jnp.where(ok, new_top, -masked_score) for ok in allowed]
            terms = jnp.concatenate(
                [jnp.exp2((piece - shift) * EXP_SCALE) for piece, shift in zip(pieces, shifts)], axis=0
            )
            total = jnp.sum(terms, axis=0, keepdims=True)
            accum = jnp.dot(values, terms.astype(bf16), preferred_element_type=f32)
            if not first:
                total = total + ins[place][HD + 1 : HD + 2, cols] * shrink
                accum = accum + ins[place][:HD, cols] * shrink
            out = outs[place]
            out[:HD, cols] = accum
            out[HD : HD + 1, cols] = new_top
            out[HD + 1 : HD + 2, cols] = total
            out[HD + 2 : STATE, cols] = jnp.zeros((STATE - HD - 2, SPAN), f32)


def attend(key_spans, query_spans, queries, blocks, key_row, states, halves=(0, 1)):
    first = states is None
    given = () if first else tuple(states[half] for half in halves)
    return pl.pallas_call(
        functools.partial(attend_kernel, first, len(blocks), key_row, halves),
        out_shape=(jax.ShapeDtypeStruct((STATE, QCOLS), f32),) * len(halves),
        in_specs=vmem(4 + len(blocks) + len(given)),
        out_specs=tuple(vmem(len(halves))),
        compiler_params=pltpu.CompilerParams(vmem_limit_bytes=ATTEND_LIMIT),
        cost_estimate=pl.CostEstimate(
            flops=16 * ROWS * len(halves) * QCOLS * HD,
            bytes_accessed=8 * ROWS * HD + 2 * STATE * QCOLS * 8,
            transcendentals=2 * ROWS * len(halves) * QCOLS,
        ),
        name="attend",
    )(key_spans, query_spans, *queries, *blocks, *given)


def finish_kernel(mine_ref, theirs_ref, out_ref):
    top_a, top_b = mine_ref[HD : HD + 1, :], theirs_ref[HD : HD + 1, :]
    top = jnp.maximum(top_a, top_b)
    scale_a = jnp.exp2((top_a - top) * EXP_SCALE)
    scale_b = jnp.exp2((top_b - top) * EXP_SCALE)
    total = mine_ref[HD + 1 : HD + 2, :] * scale_a + theirs_ref[HD + 1 : HD + 2, :] * scale_b
    accum = (mine_ref[:HD, :] * scale_a + theirs_ref[:HD, :] * scale_b) / total
    for s in range(2):
        for g in range(GROUPS):
            start = (s * GROUPS + g) * SPAN
            out_ref[s * SPAN : (s + 1) * SPAN, g * HD : (g + 1) * HD] = accum[
                :, start : start + SPAN
            ].T.astype(bf16)


def finish(mine, theirs):
    return pl.pallas_call(
        finish_kernel,
        out_shape=jax.ShapeDtypeStruct((ROWS, GROUPS * HD), bf16),
        in_specs=vmem(2),
        out_specs=pl.BlockSpec(memory_space=pltpu.VMEM),
        compiler_params=pltpu.CompilerParams(vmem_limit_bytes=VMEM_LIMIT),
        name="finish",
    )(mine, theirs)


def send_on(block, before, size, steps):
    block, unused = lax.optimization_barrier((block, before))
    return lax.ppermute(block[:size], "ctx", z_move(steps))


def on_device(patches, vis_pos, span_of, text_rows, proj_weight, norm_gain, qkv_weight):
    place = lax.axis_index("ctx")
    x_hi, z, core = place // 16, place // 2 % Z, place % 2
    weight = jnp.transpose(qkv_weight, (2, 0, 1, 3)).reshape(GROUPS + 2, HEAD_DEVS, COLS, HD)
    gain = norm_gain.reshape(HEAD_DEVS, 1, COLS)

    lanes = jnp.arange(HD, dtype=jnp.int32)[None, :]
    my_rows = pl.pallas_call(
        entry_kernel,
        out_shape=jax.ShapeDtypeStruct((OWNERS, HD), jnp.int32),
        in_specs=vmem(1),
        out_specs=pl.BlockSpec(memory_space=pltpu.VMEM),
        name="my_entry",
    )(span_of)
    table_rows = lax.all_to_all(
        my_rows.reshape(OWNERS, 1, HD), "ctx", split_axis=0, concat_axis=0, tiled=True
    ).reshape(OWNERS, HD)
    visual = jnp.dot(patches, proj_weight, preferred_element_type=f32).astype(bf16)

    taken = [(0, 0, 0)]
    for flip, hop in MESSAGES:
        taken += [(flip, hop, 0), (flip, hop, 1)]
    taken += [(1, 0, 0), (0, 4, 0), (1, 4, 0)]
    back = 2 * core - 1
    sources = [
        (((x_hi + flip) % 2) * Z + (z + back * hop + Z) % Z) * 2 + (core + turn) % 2 for flip, hop, turn in taken
    ]
    mine = place
    other = place + 1 - 2 * core
    wanted = jnp.stack([2 * source + s for source in [*sources, mine, other] for s in range(2)])
    table = jnp.sum(table_rows, axis=0)[None, :]
    spans = jnp.sum(jnp.where(wanted[:, None] == lanes, table, 0), axis=1).astype(f32)
    key_spans = jnp.broadcast_to(spans[:OWNERS, None], (OWNERS, SPAN))
    query_spans = jnp.broadcast_to(
        spans[OWNERS:].reshape(2, 2, 1), (2, 2, GROUPS * SPAN)
    ).reshape(2, QCOLS)

    row_pos = (span_of.reshape(2, 1) * SPAN + jnp.arange(SPAN, dtype=jnp.int32)[None, :]).reshape(ROWS)
    cosine, sine = rotary_tables(row_pos)

    mail = whole(route_kernel, (SLOTS, COLS + HD), "route_rows", visual, vis_pos[:, None], table_rows)
    mail = lax.all_to_all(
        mail.reshape(OWNERS, CAP, COLS + HD), "ctx", split_axis=0, concat_axis=0, tiled=True
    ).reshape(SLOTS, COLS + HD)
    sequence = whole(place_kernel, (ROWS, COLS), "place_rows", mail, text_rows)
    first = lax.optimization_barrier(gather_first(sequence))
    second = lax.optimization_barrier(gather_second(*first))
    halves = (second[2][:SPAN], second[1][SPAN:])
    weight, gain, cosine, sine, halves = lax.optimization_barrier((weight, gain, cosine, sine, halves))
    third = gather_third(*halves)
    queries, own = project_qkv(
        [sequence, *first, *second, *third], load_weight(weight), gain, cosine, sine
    )

    stream = jnp.concatenate([own, lax.ppermute(own, "ctx", core_swap())], axis=0)
    stream, queries, own = lax.optimization_barrier((stream, queries, own))
    moved = lax.ppermute(stream, "ctx", z_move())
    crossed = lax.ppermute(stream, "ctx", z_cross())
    other_queries = lax.ppermute(queries, "ctx", core_swap())
    side = lax.ppermute(own, "ctx", xhi_swap())
    step = functools.partial(attend, key_spans, query_spans, (queries, other_queries))
    states = step([own], 0, None)
    key_row = 2
    history = [states]
    held = {(0, 1): moved, (1, 1): crossed}
    for message in MESSAGES:
        for after, line, old, new in SENDS:
            if after == len(history) - 1:
                held[line, new] = send_on(held[line, old], states, 4 * ROWS if new < 4 else 2 * ROWS, new - old)
        states = step([held[message]], key_row, states)
        key_row += 4
        history.append(states)
    states = step([side], key_row, states)
    key_row += 2
    moved, crossed = held[0, 4], held[1, 4]
    (given,) = step([moved, crossed], key_row, states, (1,))
    theirs = lax.ppermute(given, "ctx", core_swap())
    (kept,) = step([moved, crossed], key_row, states, (0,))
    return finish(kept, theirs)


def solution(mesh):
    in_specs = (
        P("ctx", None),
        P("ctx"),
        P("ctx", None),
        P("ctx", "head"),
        P(None, "head"),
        P(),
        P(None, "head", None, None),
    )
    out_specs = P("ctx", "head")
    return jax.shard_map(
        on_device, mesh=mesh, in_specs=in_specs, out_specs=out_specs, check_vma=False
    )
```

```python
import functools
import math

import jax
import jax.numpy as jnp
from jax import lax
from jax.experimental import pallas as pl
from jax.experimental.pallas import tpu as pltpu
from jax.sharding import PartitionSpec as P

HEADS = 32
KVH = 8
HD = 128
GROUPS = HEADS // KVH
WIDE = (GROUPS + 2) * HD
SPAN = 128
ROWS = 2 * SPAN
OWNERS = 32
CAP = ROWS // OWNERS
SLOTS = OWNERS * CAP
Z = 8
Y = 4
HEAD_DEVS = 8
COLS = 512
MAIL = WIDE + HD
QCOLS = GROUPS * ROWS
STATE = HD + 8

MESSAGES = [(0, 1), (0, 2), (1, 1), (0, 3), (1, 2), (1, 3)]
SENDS = [(0, 0, 1, 2), (1, 0, 2, 3), (1, 1, 1, 2), (1, 1, 1, 3), (2, 0, 3, 4), (3, 1, 2, 4)]

rope_theta = 500000.0
norm_eps = 1e-05
masked_score = -1e30
EXP_SCALE = HD ** (-0.5) * math.log2(math.e)
VMEM_LIMIT = 16 * 1024 * 1024
ATTEND_LIMIT = 8 * 1024 * 1024

bf16 = jnp.bfloat16
f32 = jnp.float32


def ctx_perm(move):
    return [(i, move(i)) for i in range(OWNERS)]


def z_move(steps=1):
    return ctx_perm(lambda i: (i // 16) * 16 + ((i // 2 % Z + steps * (1 - 2 * (i % 2))) % Z) * 2 + i % 2)


def z_cross():
    return [(i, j ^ 16) for i, j in z_move()]


def core_swap():
    return ctx_perm(lambda i: i ^ 1)


def xhi_swap():
    return ctx_perm(lambda i: i ^ 16)


def y_shift(step):
    return [(i, (i // 2 + step) % Y * 2 + i % 2) for i in range(HEAD_DEVS)]


def xlo_swap():
    return [(i, i ^ 1) for i in range(HEAD_DEVS)]


def rotary_tables(positions):
    frequency = rope_theta ** (-jnp.arange(0, HD, 2, dtype=f32) / HD)
    angles = positions.astype(f32)[:, None] * frequency[None, :]
    cosine, sine = jnp.cos(angles), jnp.sin(angles)
    return jnp.concatenate([cosine, cosine], axis=1), jnp.concatenate([-sine, sine], axis=1)


def gather_first(own):
    return [
        lax.ppermute(own, "head", xlo_swap()),
        lax.ppermute(own, "head", y_shift(1)),
        lax.ppermute(own, "head", y_shift(-1)),
    ]


def gather_second(side, down, up):
    return [
        lax.ppermute(side, "head", y_shift(2)),
        lax.ppermute(down, "head", y_shift(1)),
        lax.ppermute(side, "head", y_shift(-1)),
        lax.ppermute(down, "head", xlo_swap()),
    ]


def block_order(place):
    y, x = place // 2, place % 2

    def at(step, flip):
        return (y + step + Y) % Y * 2 + (x + flip) % 2

    return [at(0, 0), at(0, 1), at(-1, 0), at(1, 0), at(2, 0), at(1, 1), at(-1, 1), at(2, 1)]


def qkv_kernel(rows, count, *refs):
    blocks, refs = refs[:count], refs[count:]
    weight_ref, gain_ref, cos_ref, sin_ref = refs[:4]
    order = block_order(lax.axis_index("head")) if count > 1 else list(range(HEAD_DEVS))

    def block(k):
        if count == 1:
            return blocks[0][:, k * COLS : (k + 1) * COLS].astype(f32)
        return blocks[k][...].astype(f32)

    squares = jnp.zeros((rows, COLS), f32)
    for k in range(8):
        wide = block(k)
        squares = squares + wide * wide
    total = jnp.sum(squares, axis=1, keepdims=True)
    inverse = lax.rsqrt(total * (1.0 / (8 * COLS)) + norm_eps)
    pairs = (GROUPS + 2) // 2
    projected = [jnp.zeros((rows, 2 * HD), f32) for pair in range(pairs)]
    for k in range(8):
        normed = (block(k) * inverse * gain_ref[order[k]]).astype(bf16)
        for pair in range(pairs):
            weight = jnp.concatenate(
                [weight_ref[2 * pair, order[k]], weight_ref[2 * pair + 1, order[k]]], axis=1
            )
            projected[pair] = projected[pair] + jnp.dot(
                normed, weight, preferred_element_type=f32
            )
    cosine, sine = cos_ref[...], sin_ref[...]
    parts = []
    for j in range(GROUPS + 2):
        slab = projected[j // 2][:, j % 2 * HD : (j % 2 + 1) * HD]
        if j <= GROUPS:
            slab = slab * cosine + pltpu.roll(slab, HD // 2, 1) * sine
        parts.append(slab)
    query_ref, kv_ref = refs[4:6]
    for j in range(GROUPS + 2):
        if j == GROUPS:
            kv_ref[:ROWS, :] = parts[j].astype(bf16)
            continue
        for s in range(2):
            turned = parts[j][s * SPAN : (s + 1) * SPAN, :].T.astype(bf16)
            if j < GROUPS:
                start = (s * GROUPS + j) * SPAN
                query_ref[:, start : start + SPAN] = turned
            else:
                kv_ref[ROWS + s * SPAN : ROWS + (s + 1) * SPAN, :] = turned


def vmem(count):
    return [pl.BlockSpec(memory_space=pltpu.VMEM)] * count


def load_kernel(weight_ref, out_ref, sems):
    copies = [
        pltpu.make_async_copy(weight_ref.at[j], out_ref.at[j], sems.at[j]) for j in range(GROUPS + 2)
    ]
    for copy in copies:
        copy.start()
    for copy in copies:
        copy.wait()


def load_weight(weight):
    return pl.pallas_call(
        load_kernel,
        out_shape=jax.ShapeDtypeStruct(weight.shape, bf16),
        in_specs=[pl.BlockSpec(memory_space=pltpu.HBM)],
        out_specs=pl.BlockSpec(memory_space=pltpu.VMEM),
        scratch_shapes=[pltpu.SemaphoreType.DMA((GROUPS + 2,))],
        compiler_params=pltpu.CompilerParams(vmem_limit_bytes=ATTEND_LIMIT),
        cost_estimate=pl.CostEstimate(flops=0, bytes_accessed=2 * weight.size * 2, transcendentals=0),
        name="load_weight",
    )(weight)


def project_qkv(blocks, weight, gain, cosine, sine):
    rows = blocks[0].shape[0]
    return pl.pallas_call(
        functools.partial(qkv_kernel, rows, len(blocks)),
        out_shape=(
            jax.ShapeDtypeStruct((HD, QCOLS), bf16),
            jax.ShapeDtypeStruct((2 * ROWS, HD), bf16),
        ),
        in_specs=vmem(len(blocks) + 4),
        out_specs=tuple(vmem(2)),
        compiler_params=pltpu.CompilerParams(vmem_limit_bytes=VMEM_LIMIT),
        cost_estimate=pl.CostEstimate(
            flops=2 * rows * 8 * COLS * WIDE, bytes_accessed=8 * COLS * WIDE * 2 + rows * 8192, transcendentals=0
        ),
        name="norm_qkv",
    )(*blocks, weight, gain, cosine, sine)


def entry_kernel(span_ref, out_ref):
    lane = lax.broadcasted_iota(jnp.int32, (OWNERS, HD), 1) - 2 * lax.axis_index("ctx")
    first = jnp.broadcast_to(span_ref[:, :1], (OWNERS, HD))
    second = jnp.broadcast_to(span_ref[:, 1:], (OWNERS, HD))
    out_ref[...] = jnp.where(lane == 0, first, jnp.where(lane == 1, second, 0))


def route_kernel(rows_ref, pos_ref, table_ref, out_ref):
    count = rows_ref.shape[0]
    lane = lax.broadcasted_iota(jnp.int32, (count, HD), 1)
    table = jnp.sum(table_ref[...].astype(f32), axis=0, keepdims=True)
    matches = (pos_ref[...] // SPAN).astype(f32) == jnp.where(lane < 2 * OWNERS, table, -1.0)
    entry = jnp.sum(jnp.where(matches, lane.astype(f32), 0.0), axis=1, keepdims=True).astype(jnp.int32)
    owner = entry // 2
    same = jnp.where(lane // 2 == owner, 1.0, 0.0).astype(bf16)
    square = (count, count)
    before = lax.broadcasted_iota(jnp.int32, square, 1) < lax.broadcasted_iota(jnp.int32, square, 0)
    ranks = jnp.dot(jnp.where(before, 1.0, 0.0).astype(bf16), same, preferred_element_type=f32)
    rank = jnp.sum(jnp.where(matches, ranks, 0.0), axis=1, keepdims=True).astype(jnp.int32)
    slot = owner * CAP + rank
    pick = jnp.where(lax.broadcasted_iota(jnp.int32, (count, SLOTS), 1) == slot, 1.0, 0.0).astype(bf16)
    mark = (entry % 2 * SPAN + pos_ref[...] % SPAN + 1).astype(f32)
    marks = jnp.broadcast_to(mark, (count, HD)).astype(bf16)
    across = (((0,), (0,)), ((), ()))
    out_ref[:, :COLS] = lax.dot_general(pick, rows_ref[...], across, preferred_element_type=f32).astype(bf16)
    out_ref[:, COLS:] = lax.dot_general(pick, marks, across, preferred_element_type=f32).astype(bf16)


def place_kernel(mail_ref, text_ref, out_ref):
    mail = mail_ref[...]
    marks = mail[:, COLS : COLS + 1].astype(f32)
    rows = (lax.broadcasted_iota(jnp.int32, (SLOTS, ROWS), 1) + 1).astype(f32)
    place = jnp.where(marks == rows, 1.0, 0.0).astype(bf16)
    placed = lax.dot_general(place, mail, (((0,), (0,)), ((), ())), preferred_element_type=f32)
    visual = placed[:, COLS:] > 0.5
    for j in range(COLS // HD):
        cols = slice(j * HD, (j + 1) * HD)
        out_ref[:, cols] = jnp.where(visual, placed[:, cols], text_ref[:, cols].astype(f32)).astype(bf16)


def whole(kernel, shape, name, *args):
    return pl.pallas_call(
        kernel,
        out_shape=jax.ShapeDtypeStruct(shape, bf16),
        in_specs=vmem(len(args)),
        out_specs=pl.BlockSpec(memory_space=pltpu.VMEM),
        compiler_params=pltpu.CompilerParams(vmem_limit_bytes=ATTEND_LIMIT),
        cost_estimate=pl.CostEstimate(flops=2 * SLOTS * ROWS * COLS, bytes_accessed=4 * ROWS * COLS, transcendentals=0),
        name=name,
    )(*args)


def attend_kernel(first, given, key_row, halves, *refs):
    key_ref, span_ref = refs[:2]
    query_refs = refs[2:4]
    kv_refs = refs[4 : 4 + given]
    ins, outs = refs[4 + given : -len(halves)], refs[-len(halves) :]
    parts = [(kv, start) for kv in kv_refs for start in range(0, kv.shape[0], 2 * ROWS)]
    keys = jnp.concatenate([kv[start : start + ROWS, :] for kv, start in parts], axis=0)
    values = jnp.concatenate(
        [kv[start + ROWS + s * SPAN : start + ROWS + (s + 1) * SPAN, :] for kv, start in parts for s in range(2)],
        axis=1,
    )
    count = 2 * len(parts)
    row = lax.broadcasted_iota(jnp.int32, (SPAN, SPAN), 0).astype(f32)
    lane = lax.broadcasted_iota(jnp.int32, (SPAN, SPAN), 1).astype(f32)
    for place, half in enumerate(halves):
        for tile in range(QCOLS // SPAN):
            cols = slice(tile * SPAN, (tile + 1) * SPAN)
            query_span = span_ref[half : half + 1, cols]
            score = jnp.dot(keys, query_refs[half][:, cols], preferred_element_type=f32)
            pieces = [score[j * SPAN : (j + 1) * SPAN, :] for j in range(count)]
            key_spans = [key_ref[key_row + j : key_row + j + 1, :] for j in range(count)]
            if first:
                pieces = [
                    jnp.where(span * SPAN + row <= query_span * SPAN + lane, piece, masked_score)
                    for span, piece in zip(key_spans, pieces)
                ]
                new_top = functools.reduce(
                    jnp.maximum, [jnp.max(piece, axis=0, keepdims=True) for piece in pieces]
                )
                shifts = [new_top] * count
            else:
                top = ins[place][HD : HD + 1, cols]
                allowed = [span < query_span for span in key_spans]
                highs = [
                    jnp.where(ok, jnp.max(piece, axis=0, keepdims=True), masked_score)
                    for ok, piece in zip(allowed, pieces)
                ]
                new_top = functools.reduce(jnp.maximum, highs, top)
                shrink = jnp.exp2((top - new_top) * EXP_SCALE)
                shifts = [jnp.where(ok, new_top, -masked_score) for ok in allowed]
            terms = jnp.concatenate(
                [jnp.exp2((piece - shift) * EXP_SCALE) for piece, shift in zip(pieces, shifts)], axis=0
            )
            total = jnp.sum(terms, axis=0, keepdims=True)
            accum = jnp.dot(values, terms.astype(bf16), preferred_element_type=f32)
            if not first:
                total = total + ins[place][HD + 1 : HD + 2, cols] * shrink
                accum = accum + ins[place][:HD, cols] * shrink
            out = outs[place]
            out[:HD, cols] = accum
            out[HD : HD + 1, cols] = new_top
            out[HD + 1 : HD + 2, cols] = total
            out[HD + 2 : STATE, cols] = jnp.zeros((STATE - HD - 2, SPAN), f32)


def attend(key_spans, query_spans, queries, blocks, key_row, states, halves=(0, 1)):
    first = states is None
    given = () if first else tuple(states[half] for half in halves)
    return pl.pallas_call(
        functools.partial(attend_kernel, first, len(blocks), key_row, halves),
        out_shape=(jax.ShapeDtypeStruct((STATE, QCOLS), f32),) * len(halves),
        in_specs=vmem(4 + len(blocks) + len(given)),
        out_specs=tuple(vmem(len(halves))),
        compiler_params=pltpu.CompilerParams(vmem_limit_bytes=ATTEND_LIMIT),
        cost_estimate=pl.CostEstimate(
            flops=16 * ROWS * len(halves) * QCOLS * HD,
            bytes_accessed=8 * ROWS * HD + 2 * STATE * QCOLS * 8,
            transcendentals=2 * ROWS * len(halves) * QCOLS,
        ),
        name="attend",
    )(key_spans, query_spans, *queries, *blocks, *given)


def finish_kernel(mine_ref, theirs_ref, out_ref):
    top_a, top_b = mine_ref[HD : HD + 1, :], theirs_ref[HD : HD + 1, :]
    top = jnp.maximum(top_a, top_b)
    scale_a = jnp.exp2((top_a - top) * EXP_SCALE)
    scale_b = jnp.exp2((top_b - top) * EXP_SCALE)
    total = mine_ref[HD + 1 : HD + 2, :] * scale_a + theirs_ref[HD + 1 : HD + 2, :] * scale_b
    accum = (mine_ref[:HD, :] * scale_a + theirs_ref[:HD, :] * scale_b) / total
    for s in range(2):
        for g in range(GROUPS):
            start = (s * GROUPS + g) * SPAN
            out_ref[s * SPAN : (s + 1) * SPAN, g * HD : (g + 1) * HD] = accum[
                :, start : start + SPAN
            ].T.astype(bf16)


def finish(mine, theirs):
    return pl.pallas_call(
        finish_kernel,
        out_shape=jax.ShapeDtypeStruct((ROWS, GROUPS * HD), bf16),
        in_specs=vmem(2),
        out_specs=pl.BlockSpec(memory_space=pltpu.VMEM),
        compiler_params=pltpu.CompilerParams(vmem_limit_bytes=VMEM_LIMIT),
        name="finish",
    )(mine, theirs)


def send_on(block, before, size, steps):
    block, unused = lax.optimization_barrier((block, before))
    return lax.ppermute(block[:size], "ctx", z_move(steps))


def on_device(patches, vis_pos, span_of, text_rows, proj_weight, norm_gain, qkv_weight):
    place = lax.axis_index("ctx")
    x_hi, z, core = place // 16, place // 2 % Z, place % 2
    weight = jnp.transpose(qkv_weight, (2, 0, 1, 3)).reshape(GROUPS + 2, HEAD_DEVS, COLS, HD)
    gain = norm_gain.reshape(HEAD_DEVS, 1, COLS)

    lanes = jnp.arange(HD, dtype=jnp.int32)[None, :]
    my_rows = pl.pallas_call(
        entry_kernel,
        out_shape=jax.ShapeDtypeStruct((OWNERS, HD), jnp.int32),
        in_specs=vmem(1),
        out_specs=pl.BlockSpec(memory_space=pltpu.VMEM),
        name="my_entry",
    )(span_of)
    table_rows = lax.all_to_all(
        my_rows.reshape(OWNERS, 1, HD), "ctx", split_axis=0, concat_axis=0, tiled=True
    ).reshape(OWNERS, HD)
    visual = jnp.dot(patches, proj_weight, preferred_element_type=f32).astype(bf16)

    taken = [(0, 0, 0)]
    for flip, hop in MESSAGES:
        taken += [(flip, hop, 0), (flip, hop, 1)]
    taken += [(1, 0, 0), (0, 4, 0), (1, 4, 0)]
    back = 2 * core - 1
    sources = [
        (((x_hi + flip) % 2) * Z + (z + back * hop + Z) % Z) * 2 + (core + turn) % 2 for flip, hop, turn in taken
    ]
    mine = place
    other = place + 1 - 2 * core
    wanted = jnp.stack([2 * source + s for source in [*sources, mine, other] for s in range(2)])
    table = jnp.sum(table_rows, axis=0)[None, :]
    spans = jnp.sum(jnp.where(wanted[:, None] == lanes, table, 0), axis=1).astype(f32)
    key_spans = jnp.broadcast_to(spans[:OWNERS, None], (OWNERS, SPAN))
    query_spans = jnp.broadcast_to(
        spans[OWNERS:].reshape(2, 2, 1), (2, 2, GROUPS * SPAN)
    ).reshape(2, QCOLS)

    row_pos = (span_of.reshape(2, 1) * SPAN + jnp.arange(SPAN, dtype=jnp.int32)[None, :]).reshape(ROWS)
    cosine, sine = rotary_tables(row_pos)

    mail = whole(route_kernel, (SLOTS, COLS + HD), "route_rows", visual, vis_pos[:, None], table_rows)
    mail = lax.all_to_all(
        mail.reshape(OWNERS, CAP, COLS + HD), "ctx", split_axis=0, concat_axis=0, tiled=True
    ).reshape(SLOTS, COLS + HD)
    sequence = whole(place_kernel, (ROWS, COLS), "place_rows", mail, text_rows)
    first = lax.optimization_barrier(gather_first(sequence))
    weight, gain, cosine, sine, first = lax.optimization_barrier((weight, gain, cosine, sine, first))
    far_side, far, side_up, side_down = gather_second(*first)
    queries, own = project_qkv(
        [sequence, *first, far, side_up, side_down, far_side], load_weight(weight), gain, cosine, sine
    )

    stream = jnp.concatenate([own, lax.ppermute(own, "ctx", core_swap())], axis=0)
    stream, queries, own = lax.optimization_barrier((stream, queries, own))
    moved = lax.ppermute(stream, "ctx", z_move())
    crossed = lax.ppermute(stream, "ctx", z_cross())
    other_queries = lax.ppermute(queries, "ctx", core_swap())
    side = lax.ppermute(own, "ctx", xhi_swap())
    step = functools.partial(attend, key_spans, query_spans, (queries, other_queries))
    states = step([own], 0, None)
    key_row = 2
    history = [states]
    held = {(0, 1): moved, (1, 1): crossed}
    for message in MESSAGES:
        for after, line, old, new in SENDS:
            if after == len(history) - 1:
                held[line, new] = send_on(held[line, old], states, 4 * ROWS if new < 4 else 2 * ROWS, new - old)
        states = step([held[message]], key_row, states)
        key_row += 4
        history.append(states)
    states = step([side], key_row, states)
    key_row += 2
    moved, crossed = held[0, 4], held[1, 4]
    (given,) = step([moved, crossed], key_row, states, (1,))
    theirs = lax.ppermute(given, "ctx", core_swap())
    (kept,) = step([moved, crossed], key_row, states, (0,))
    return finish(kept, theirs)


def solution(mesh):
    in_specs = (
        P("ctx", None),
        P("ctx"),
        P("ctx", None),
        P("ctx", "head"),
        P(None, "head"),
        P(),
        P(None, "head", None, None),
    )
    out_specs = P("ctx", "head")
    return jax.shard_map(
        on_device, mesh=mesh, in_specs=in_specs, out_specs=out_specs, check_vma=False
    )
```

```python
import functools
import math

import jax
import jax.numpy as jnp
from jax import lax
from jax.experimental import pallas as pl
from jax.experimental.pallas import tpu as pltpu
from jax.sharding import PartitionSpec as P

HEADS = 32
KVH = 8
HD = 128
GROUPS = HEADS // KVH
WIDE = (GROUPS + 2) * HD
SPAN = 128
ROWS = 2 * SPAN
OWNERS = 32
CAP = ROWS // OWNERS
SLOTS = OWNERS * CAP
Z = 8
Y = 4
HEAD_DEVS = 8
COLS = 512
MAIL = WIDE + HD
QCOLS = GROUPS * ROWS
STATE = HD + 8

MESSAGES = [(0, 1), (0, 2), (1, 1), (0, 3), (1, 2), (1, 3)]
SENDS = [(0, 0, 1, 2), (1, 0, 2, 3), (1, 1, 1, 2), (3, 1, 2, 3), (2, 0, 3, 4), (3, 1, 2, 4)]

rope_theta = 500000.0
norm_eps = 1e-05
masked_score = -1e30
EXP_SCALE = HD ** (-0.5) * math.log2(math.e)
VMEM_LIMIT = 16 * 1024 * 1024
ATTEND_LIMIT = 8 * 1024 * 1024

bf16 = jnp.bfloat16
f32 = jnp.float32


def ctx_perm(move):
    return [(i, move(i)) for i in range(OWNERS)]


def z_move(steps=1):
    return ctx_perm(lambda i: (i // 16) * 16 + ((i // 2 % Z + steps * (1 - 2 * (i % 2))) % Z) * 2 + i % 2)


def z_cross():
    return [(i, j ^ 16) for i, j in z_move()]


def core_swap():
    return ctx_perm(lambda i: i ^ 1)


def xhi_swap():
    return ctx_perm(lambda i: i ^ 16)


def y_shift(step):
    return [(i, (i // 2 + step) % Y * 2 + i % 2) for i in range(HEAD_DEVS)]


def xlo_swap():
    return [(i, i ^ 1) for i in range(HEAD_DEVS)]


def rotary_tables(positions):
    frequency = rope_theta ** (-jnp.arange(0, HD, 2, dtype=f32) / HD)
    angles = positions.astype(f32)[:, None] * frequency[None, :]
    cosine, sine = jnp.cos(angles), jnp.sin(angles)
    return jnp.concatenate([cosine, cosine], axis=1), jnp.concatenate([-sine, sine], axis=1)


def gather_blocks(own):
    side = lax.ppermute(own, "head", xlo_swap())
    down = lax.ppermute(own, "head", y_shift(1))
    up = lax.ppermute(own, "head", y_shift(-1))
    far_side = lax.ppermute(side, "head", y_shift(2))
    down, up = lax.optimization_barrier((down, up))
    far = lax.ppermute(down, "head", y_shift(1))
    side_up = lax.ppermute(up, "head", xlo_swap())
    side_down = lax.ppermute(down, "head", xlo_swap())
    return [own, side, down, up, far, side_up, side_down, far_side]


def block_order(place):
    y, x = place // 2, place % 2

    def at(step, flip):
        return (y + step + Y) % Y * 2 + (x + flip) % 2

    return [at(0, 0), at(0, 1), at(-1, 0), at(1, 0), at(2, 0), at(1, 1), at(-1, 1), at(2, 1)]


def qkv_kernel(rows, *refs):
    blocks = refs[:HEAD_DEVS]
    weight_ref, gain_ref, cos_ref, sin_ref, query_ref, kv_ref = refs[HEAD_DEVS:]
    order = block_order(lax.axis_index("head"))

    def block(k):
        return blocks[k][...].astype(f32)

    squares = jnp.zeros((rows, COLS), f32)
    for k in range(8):
        wide = block(k)
        squares = squares + wide * wide
    total = jnp.sum(squares, axis=1, keepdims=True)
    inverse = lax.rsqrt(total * (1.0 / (8 * COLS)) + norm_eps)
    pairs = (GROUPS + 2) // 2
    projected = [jnp.zeros((rows, 2 * HD), f32) for pair in range(pairs)]
    for k in range(8):
        normed = (block(k) * inverse * gain_ref[order[k]]).astype(bf16)
        for pair in range(pairs):
            weight = jnp.concatenate(
                [weight_ref[2 * pair, order[k]], weight_ref[2 * pair + 1, order[k]]], axis=1
            )
            projected[pair] = projected[pair] + jnp.dot(
                normed, weight, preferred_element_type=f32
            )
    cosine, sine = cos_ref[...], sin_ref[...]
    parts = []
    for j in range(GROUPS + 2):
        slab = projected[j // 2][:, j % 2 * HD : (j % 2 + 1) * HD]
        if j <= GROUPS:
            slab = slab * cosine + pltpu.roll(slab, HD // 2, 1) * sine
        parts.append(slab)
    for j in range(GROUPS + 2):
        if j == GROUPS:
            kv_ref[:ROWS, :] = parts[j].astype(bf16)
            continue
        for s in range(2):
            turned = parts[j][s * SPAN : (s + 1) * SPAN, :].T.astype(bf16)
            if j < GROUPS:
                start = (s * GROUPS + j) * SPAN
                query_ref[:, start : start + SPAN] = turned
            else:
                kv_ref[ROWS + s * SPAN : ROWS + (s + 1) * SPAN, :] = turned


def vmem(count):
    return [pl.BlockSpec(memory_space=pltpu.VMEM)] * count


def load_kernel(weight_ref, out_ref, sems):
    copies = [
        pltpu.make_async_copy(weight_ref.at[j], out_ref.at[j], sems.at[j]) for j in range(GROUPS + 2)
    ]
    for copy in copies:
        copy.start()
    for copy in copies:
        copy.wait()


def load_weight(weight):
    return pl.pallas_call(
        load_kernel,
        out_shape=jax.ShapeDtypeStruct(weight.shape, bf16),
        in_specs=[pl.BlockSpec(memory_space=pltpu.HBM)],
        out_specs=pl.BlockSpec(memory_space=pltpu.VMEM),
        scratch_shapes=[pltpu.SemaphoreType.DMA((GROUPS + 2,))],
        compiler_params=pltpu.CompilerParams(vmem_limit_bytes=ATTEND_LIMIT),
        cost_estimate=pl.CostEstimate(flops=0, bytes_accessed=2 * weight.size * 2, transcendentals=0),
        name="load_weight",
    )(weight)


def project_qkv(blocks, weight, gain, cosine, sine):
    rows = blocks[0].shape[0]
    return pl.pallas_call(
        functools.partial(qkv_kernel, rows),
        out_shape=(
            jax.ShapeDtypeStruct((HD, QCOLS), bf16),
            jax.ShapeDtypeStruct((2 * ROWS, HD), bf16),
        ),
        in_specs=vmem(len(blocks) + 4),
        out_specs=tuple(vmem(2)),
        compiler_params=pltpu.CompilerParams(vmem_limit_bytes=VMEM_LIMIT),
        cost_estimate=pl.CostEstimate(
            flops=2 * rows * 8 * COLS * WIDE, bytes_accessed=8 * COLS * WIDE * 2 + rows * 8192, transcendentals=0
        ),
        name="norm_qkv",
    )(*blocks, weight, gain, cosine, sine)


def entry_kernel(span_ref, out_ref):
    lane = lax.broadcasted_iota(jnp.int32, (OWNERS, HD), 1) - 2 * lax.axis_index("ctx")
    first = jnp.broadcast_to(span_ref[:, :1], (OWNERS, HD))
    second = jnp.broadcast_to(span_ref[:, 1:], (OWNERS, HD))
    out_ref[...] = jnp.where(lane == 0, first, jnp.where(lane == 1, second, 0))


def route_kernel(rows_ref, pos_ref, table_ref, out_ref):
    count = rows_ref.shape[0]
    lane = lax.broadcasted_iota(jnp.int32, (count, HD), 1)
    table = jnp.sum(table_ref[...].astype(f32), axis=0, keepdims=True)
    matches = (pos_ref[...] // SPAN).astype(f32) == jnp.where(lane < 2 * OWNERS, table, -1.0)
    entry = jnp.sum(jnp.where(matches, lane.astype(f32), 0.0), axis=1, keepdims=True).astype(jnp.int32)
    owner = entry // 2
    same = jnp.where(lane // 2 == owner, 1.0, 0.0).astype(bf16)
    square = (count, count)
    before = lax.broadcasted_iota(jnp.int32, square, 1) < lax.broadcasted_iota(jnp.int32, square, 0)
    ranks = jnp.dot(jnp.where(before, 1.0, 0.0).astype(bf16), same, preferred_element_type=f32)
    rank = jnp.sum(jnp.where(matches, ranks, 0.0), axis=1, keepdims=True).astype(jnp.int32)
    slot = owner * CAP + rank
    pick = jnp.where(lax.broadcasted_iota(jnp.int32, (count, SLOTS), 1) == slot, 1.0, 0.0).astype(bf16)
    mark = (entry % 2 * SPAN + pos_ref[...] % SPAN + 1).astype(f32)
    marks = jnp.broadcast_to(mark, (count, HD)).astype(bf16)
    across = (((0,), (0,)), ((), ()))
    out_ref[:, :COLS] = lax.dot_general(pick, rows_ref[...], across, preferred_element_type=f32).astype(bf16)
    out_ref[:, COLS:] = lax.dot_general(pick, marks, across, preferred_element_type=f32).astype(bf16)


def place_kernel(mail_ref, text_ref, out_ref):
    mail = mail_ref[...]
    marks = mail[:, COLS : COLS + 1].astype(f32)
    rows = (lax.broadcasted_iota(jnp.int32, (SLOTS, ROWS), 1) + 1).astype(f32)
    place = jnp.where(marks == rows, 1.0, 0.0).astype(bf16)
    placed = lax.dot_general(place, mail, (((0,), (0,)), ((), ())), preferred_element_type=f32)
    visual = placed[:, COLS:] > 0.5
    for j in range(COLS // HD):
        cols = slice(j * HD, (j + 1) * HD)
        out_ref[:, cols] = jnp.where(visual, placed[:, cols], text_ref[:, cols].astype(f32)).astype(bf16)


def whole(kernel, shape, name, *args):
    return pl.pallas_call(
        kernel,
        out_shape=jax.ShapeDtypeStruct(shape, bf16),
        in_specs=vmem(len(args)),
        out_specs=pl.BlockSpec(memory_space=pltpu.VMEM),
        compiler_params=pltpu.CompilerParams(vmem_limit_bytes=ATTEND_LIMIT),
        cost_estimate=pl.CostEstimate(flops=2 * SLOTS * ROWS * COLS, bytes_accessed=4 * ROWS * COLS, transcendentals=0),
        name=name,
    )(*args)


def attend_kernel(first, given, key_row, halves, *refs):
    key_ref, span_ref = refs[:2]
    query_refs = refs[2:4]
    kv_refs = refs[4 : 4 + given]
    ins, outs = refs[4 + given : -len(halves)], refs[-len(halves) :]
    parts = [(kv, start) for kv in kv_refs for start in range(0, kv.shape[0], 2 * ROWS)]
    keys = jnp.concatenate([kv[start : start + ROWS, :] for kv, start in parts], axis=0)
    values = jnp.concatenate(
        [kv[start + ROWS + s * SPAN : start + ROWS + (s + 1) * SPAN, :] for kv, start in parts for s in range(2)],
        axis=1,
    )
    count = 2 * len(parts)
    row = lax.broadcasted_iota(jnp.int32, (SPAN, SPAN), 0).astype(f32)
    lane = lax.broadcasted_iota(jnp.int32, (SPAN, SPAN), 1).astype(f32)
    for place, half in enumerate(halves):
        for tile in range(QCOLS // SPAN):
            cols = slice(tile * SPAN, (tile + 1) * SPAN)
            query_span = span_ref[half : half + 1, cols]
            score = jnp.dot(keys, query_refs[half][:, cols], preferred_element_type=f32)
            pieces = [score[j * SPAN : (j + 1) * SPAN, :] for j in range(count)]
            key_spans = [key_ref[key_row + j : key_row + j + 1, :] for j in range(count)]
            if first:
                pieces = [
                    jnp.where(span * SPAN + row <= query_span * SPAN + lane, piece, masked_score)
                    for span, piece in zip(key_spans, pieces)
                ]
                new_top = functools.reduce(
                    jnp.maximum, [jnp.max(piece, axis=0, keepdims=True) for piece in pieces]
                )
                shifts = [new_top] * count
            else:
                top = ins[place][HD : HD + 1, cols]
                allowed = [span < query_span for span in key_spans]
                highs = [
                    jnp.where(ok, jnp.max(piece, axis=0, keepdims=True), masked_score)
                    for ok, piece in zip(allowed, pieces)
                ]
                new_top = functools.reduce(jnp.maximum, highs, top)
                shrink = jnp.exp2((top - new_top) * EXP_SCALE)
                shifts = [jnp.where(ok, new_top, -masked_score) for ok in allowed]
            terms = jnp.concatenate(
                [jnp.exp2((piece - shift) * EXP_SCALE) for piece, shift in zip(pieces, shifts)], axis=0
            )
            total = jnp.sum(terms, axis=0, keepdims=True)
            accum = jnp.dot(values, terms.astype(bf16), preferred_element_type=f32)
            if not first:
                total = total + ins[place][HD + 1 : HD + 2, cols] * shrink
                accum = accum + ins[place][:HD, cols] * shrink
            out = outs[place]
            out[:HD, cols] = accum
            out[HD : HD + 1, cols] = new_top
            out[HD + 1 : HD + 2, cols] = total
            out[HD + 2 : STATE, cols] = jnp.zeros((STATE - HD - 2, SPAN), f32)


def attend(key_spans, query_spans, queries, blocks, key_row, states, halves=(0, 1)):
    first = states is None
    given = () if first else tuple(states[half] for half in halves)
    return pl.pallas_call(
        functools.partial(attend_kernel, first, len(blocks), key_row, halves),
        out_shape=(jax.ShapeDtypeStruct((STATE, QCOLS), f32),) * len(halves),
        in_specs=vmem(4 + len(blocks) + len(given)),
        out_specs=tuple(vmem(len(halves))),
        compiler_params=pltpu.CompilerParams(vmem_limit_bytes=ATTEND_LIMIT),
        cost_estimate=pl.CostEstimate(
            flops=16 * ROWS * len(halves) * QCOLS * HD,
            bytes_accessed=8 * ROWS * HD + 2 * STATE * QCOLS * 8,
            transcendentals=2 * ROWS * len(halves) * QCOLS,
        ),
        name="attend",
    )(key_spans, query_spans, *queries, *blocks, *given)


def finish_kernel(mine_ref, theirs_ref, out_ref):
    top_a, top_b = mine_ref[HD : HD + 1, :], theirs_ref[HD : HD + 1, :]
    top = jnp.maximum(top_a, top_b)
    scale_a = jnp.exp2((top_a - top) * EXP_SCALE)
    scale_b = jnp.exp2((top_b - top) * EXP_SCALE)
    total = mine_ref[HD + 1 : HD + 2, :] * scale_a + theirs_ref[HD + 1 : HD + 2, :] * scale_b
    accum = (mine_ref[:HD, :] * scale_a + theirs_ref[:HD, :] * scale_b) / total
    for s in range(2):
        for g in range(GROUPS):
            start = (s * GROUPS + g) * SPAN
            out_ref[s * SPAN : (s + 1) * SPAN, g * HD : (g + 1) * HD] = accum[
                :, start : start + SPAN
            ].T.astype(bf16)


def finish(mine, theirs):
    return pl.pallas_call(
        finish_kernel,
        out_shape=jax.ShapeDtypeStruct((ROWS, GROUPS * HD), bf16),
        in_specs=vmem(2),
        out_specs=pl.BlockSpec(memory_space=pltpu.VMEM),
        compiler_params=pltpu.CompilerParams(vmem_limit_bytes=VMEM_LIMIT),
        name="finish",
    )(mine, theirs)


def send_on(block, before, size, steps):
    block, unused = lax.optimization_barrier((block, before))
    return lax.ppermute(block[:size], "ctx", z_move(steps))


def on_device(patches, vis_pos, span_of, text_rows, proj_weight, norm_gain, qkv_weight):
    place = lax.axis_index("ctx")
    x_hi, z, core = place // 16, place // 2 % Z, place % 2
    weight = jnp.transpose(qkv_weight, (2, 0, 1, 3)).reshape(GROUPS + 2, HEAD_DEVS, COLS, HD)
    gain = norm_gain.reshape(HEAD_DEVS, 1, COLS)

    lanes = jnp.arange(HD, dtype=jnp.int32)[None, :]
    my_rows = pl.pallas_call(
        entry_kernel,
        out_shape=jax.ShapeDtypeStruct((OWNERS, HD), jnp.int32),
        in_specs=vmem(1),
        out_specs=pl.BlockSpec(memory_space=pltpu.VMEM),
        compiler_params=pltpu.CompilerParams(vmem_limit_bytes=ATTEND_LIMIT),
        name="my_entry",
    )(span_of)
    table_rows = lax.all_to_all(
        my_rows.reshape(OWNERS, 1, HD), "ctx", split_axis=0, concat_axis=0, tiled=True
    ).reshape(OWNERS, HD)
    visual = jnp.dot(patches, proj_weight, preferred_element_type=f32).astype(bf16)

    taken = [(0, 0, 0)]
    for flip, hop in MESSAGES:
        taken += [(flip, hop, 0), (flip, hop, 1)]
    taken += [(1, 0, 0), (0, 4, 0), (1, 4, 0)]
    back = 2 * core - 1
    sources = [
        (((x_hi + flip) % 2) * Z + (z + back * hop + Z) % Z) * 2 + (core + turn) % 2 for flip, hop, turn in taken
    ]
    mine = place
    other = place + 1 - 2 * core
    wanted = jnp.stack([2 * source + s for source in [*sources, mine, other] for s in range(2)])
    table = jnp.sum(table_rows, axis=0)[None, :]
    spans = jnp.sum(jnp.where(wanted[:, None] == lanes, table, 0), axis=1).astype(f32)
    key_spans = jnp.broadcast_to(spans[:OWNERS, None], (OWNERS, SPAN))
    query_spans = jnp.broadcast_to(
        spans[OWNERS:].reshape(2, 2, 1), (2, 2, GROUPS * SPAN)
    ).reshape(2, QCOLS)

    row_pos = (span_of.reshape(2, 1) * SPAN + jnp.arange(SPAN, dtype=jnp.int32)[None, :]).reshape(ROWS)
    cosine, sine = rotary_tables(row_pos)

    mail = whole(route_kernel, (SLOTS, COLS + HD), "route_rows", visual, vis_pos[:, None], table_rows)
    mail = lax.all_to_all(
        mail.reshape(OWNERS, CAP, COLS + HD), "ctx", split_axis=0, concat_axis=0, tiled=True
    ).reshape(SLOTS, COLS + HD)
    sequence = whole(place_kernel, (ROWS, COLS), "place_rows", mail, text_rows)
    blocks = gather_blocks(sequence)
    weight, gain, cosine, sine, blocks[3] = lax.optimization_barrier((weight, gain, cosine, sine, blocks[3]))
    queries, own = project_qkv(blocks, load_weight(weight), gain, cosine, sine)

    stream = jnp.concatenate([own, lax.ppermute(own, "ctx", core_swap())], axis=0)
    stream, queries, own = lax.optimization_barrier((stream, queries, own))
    moved = lax.ppermute(stream, "ctx", z_move())
    crossed = lax.ppermute(stream, "ctx", z_cross())
    other_queries = lax.ppermute(queries, "ctx", core_swap())
    side = lax.ppermute(own, "ctx", xhi_swap())
    step = functools.partial(attend, key_spans, query_spans, (queries, other_queries))
    states = step([own], 0, None)
    key_row = 2
    history = [states]
    held = {(0, 1): moved, (1, 1): crossed}
    for message in MESSAGES:
        for after, line, old, new in SENDS:
            if after == len(history) - 1:
                held[line, new] = send_on(held[line, old], states, 4 * ROWS if new < 4 else 2 * ROWS, new - old)
        states = step([held[message]], key_row, states)
        key_row += 4
        history.append(states)
    states = step([side], key_row, states)
    key_row += 2
    moved, crossed = held[0, 4], held[1, 4]
    (given,) = step([moved, crossed], key_row, states, (1,))
    theirs = lax.ppermute(given, "ctx", core_swap())
    (kept,) = step([moved, crossed], key_row, states, (0,))
    return finish(kept, theirs)


def solution(mesh):
    in_specs = (
        P("ctx", None),
        P("ctx"),
        P("ctx", None),
        P("ctx", "head"),
        P(None, "head"),
        P(),
        P(None, "head", None, None),
    )
    out_specs = P("ctx", "head")
    return jax.shard_map(
        on_device, mesh=mesh, in_specs=in_specs, out_specs=out_specs, check_vma=False
    )
```
